256 devices in a mesh: dp: 32 (over z, y_lo, core), tensor: 8 (over y_hi, x).
Axes of the slice: x: 4, y: 4 (y_hi: 2, y_lo: 2; y = y_hi * 2 + y_lo), z: 8, core: 2. Of those that a mesh axis runs over, the one named last changes fastest.
Arguments:
- rollout_q: bfloat16 [34048, 4096], P('dp', 'tensor'), may hold values from -60 to 60
- rollout_k: bfloat16 [34048, 1024], P('dp', 'tensor'), may hold values from -8 to 8
- rollout_value_rows: bfloat16 [34048, 1024], P('dp', 'tensor'), may hold values from -6 to 6
- q_gain: float32 [128], replicated, may hold values from 0.5 to 6
- k_gain: float32 [128], replicated, may hold values from 0.5 to 6
- out_weight: bfloat16 [5120, 4096], P('dp', 'tensor'), may hold values from -0.09375 to 0.09375
- cotangent: bfloat16 [21504, 5120], P('dp', 'tensor'), may hold values from -6 to 6
- seq_lengths: int32 [192], replicated, may hold values from 28 to 196, as said below
- seq_source: int32 [192], replicated, may hold values from 0 to 31, as said below
Outputs:
- layer_out: bfloat16 [21504, 5120], P('dp', 'tensor')
- query_grad: bfloat16 [21504, 4096], P('dp', 'tensor')
- key_grad: bfloat16 [21504, 1024], P('dp', 'tensor')
- packed_value_gradient: bfloat16 [21504, 1024], P('dp', 'tensor')
- weight_grad: float32 [5120, 4096], P('dp', 'tensor')
The draws below stay inside these ranges and needn't reach their ends.
Inputs may be any that keep to these rules, and one draw needn't show every extreme that they name: `seq_lengths`: the 6 rollouts of each data shard hold exactly 672 tokens together. `seq_source`: never falling along the rollouts. A source holds the rollouts of its own shard and at most the last rollout of the shard before it and the first of the shard after it; its rollouts lie end to end from its first row in order, and at least one source holds exactly 1064 tokens in every draw.
All inputs are finite; a program needn't handle non-finite values.
Results may differ from the reference program's by a relative error of at most 0.029.
The reference program's roundings to bfloat16 on the way count: a program that leaves them out, or rounds other values in their place, can miss the bound.
Values may be sent and summed in bfloat16 or wider, within the bound.
No kernel may reach another device: no remote copies, remote signals or barrier semaphores. Data moves between devices by JAX's collectives and lax.ppermute only.
A program may use at most 128 MiB of HBM per device.

```python
import math
import jax
import jax.numpy as jnp
from jax import lax

D = 5120
QUERY_HEADS = 32
KEY_HEADS = 8
HEAD_SIZE = 128
MEAN_LEN = 112
SEQ_DEV = 6
TOK_DEV = 672
SOURCE_ROWS = 1064
NSEQ = 192
TOKENS = 21504
N_DP = 32
N_TENSOR = 8


def packing_layout(key):
    key = jax.random.fold_in(key, 500)
    leading_key, second, third_key = jax.random.split(key, 3)
    spread = 3 * MEAN_LEN // 4
    nudges = jax.random.randint(leading_key, (N_DP, SEQ_DEV), 0, spread + 1)
    boundary_moves = jax.random.randint(second, (N_DP,), -1, 2)
    chosen = jax.random.randint(third_key, (), 1, N_DP - 1)
    shard_ids = jnp.arange(N_DP)
    column = jnp.arange(SEQ_DEV)[None, :]
    boundary_moves = jnp.where(shard_ids == chosen - 1, -1, jnp.where(shard_ids == chosen, 1, boundary_moves))
    before = shard_ids[:, None] == chosen - 1
    after_pick = shard_ids[:, None] == chosen + 1
    nudges = jnp.where(before & (column == SEQ_DEV - 1), spread, nudges)
    nudges = jnp.where(before & (column == 0), 0, nudges)
    nudges = jnp.where(after_pick & (column == 0), spread, nudges)
    nudges = jnp.where(after_pick & (column == 1), 0, nudges)
    lengths = MEAN_LEN + nudges - jnp.roll(nudges, -1, axis=1)
    cut_points = (shard_ids[:-1] + 1) * SEQ_DEV + boundary_moves[:-1]
    seq_ids = jnp.arange(N_DP * SEQ_DEV)
    source = jnp.sum((seq_ids[:, None] >= cut_points[None, :]).astype(jnp.int32), axis=1)
    return (lengths.reshape(-1).astype(jnp.int32), source.astype(jnp.int32))


def shared_keys(key):
    key = jax.random.fold_in(key, 600)
    leading_key = jax.random.fold_in(key, 0)
    starting_rows = jnp.clip(jax.random.normal(leading_key, (N_DP * SOURCE_ROWS, KEY_HEADS, HEAD_SIZE), jnp.float32), -6.0, 6.0)
    return starting_rows


def draw_seq_lengths(key, part):
    lengths, source = packing_layout(key)
    return lengths


def draw_seq_source(key, part):
    lengths, source = packing_layout(key)
    return source


def draw_rollout_q(key, part):
    key = jax.random.fold_in(key, 2)
    leading_key, second = jax.random.split(key)
    queries_per_group = QUERY_HEADS // KEY_HEADS
    row_sum_total = N_DP * SOURCE_ROWS
    random_rows = jnp.clip(jax.random.normal(leading_key, (row_sum_total, KEY_HEADS, queries_per_group, HEAD_SIZE), jnp.float32), -6.0, 6.0)
    row_scale = jnp.exp(jax.random.uniform(second, (row_sum_total, 1, 1, 1), jnp.float32, 0.0, math.log(10.0)))
    value_rows = random_rows * row_scale
    return value_rows.reshape(row_sum_total, QUERY_HEADS * HEAD_SIZE).astype(jnp.bfloat16)


def draw_rollout_k(key, part):
    starting_rows = shared_keys(key)
    value_rows = starting_rows
    return value_rows.reshape(N_DP * SOURCE_ROWS, KEY_HEADS * HEAD_SIZE).astype(jnp.bfloat16)


def draw_q_gain(key, part):
    key = jax.random.fold_in(key, 4)
    return jnp.exp(jax.random.uniform(key, (HEAD_SIZE,), jnp.float32, math.log(0.5), math.log(2.0)))


def draw_k_gain(key, part):
    key = jax.random.fold_in(key, 5)
    return jnp.exp(jax.random.uniform(key, (HEAD_SIZE,), jnp.float32, math.log(0.5), math.log(2.0)))


def spiked(result, own_key, source, target, parts, factor):
    owner, partner = [(jnp.arange(result.shape[dim]) // (result.shape[dim] // parts)).reshape([-1 if axis == dim else 1 for axis in range(result.ndim)]) for dim in (source, target)]
    chosen = jax.random.permutation(own_key, parts)[partner]
    strong = (owner == chosen) | (owner == (partner + parts // 2) % parts)
    return jnp.where(strong, factor * result, result)


def shard_levels(stream_key, dims, pieces, low, top_value):
    def one(dim, shards_of):
        heights = jax.random.uniform(jax.random.fold_in(jax.random.fold_in(stream_key, 6), dim), (shards_of,), jnp.float32, low / len(pieces), top_value / len(pieces))
        return jnp.repeat(jnp.exp(heights), dims[dim] // shards_of).reshape((-1,) + (1,) * (len(dims) - dim - 1))

    level = one(*pieces[0])
    for cut in pieces[1:]:
        level = level * one(*cut)
    return level


def bell_draw(own_key, shape, deviation, bound, pieces=(), held_as=jnp.bfloat16):
    drawn = jax.random.normal(own_key, shape, jnp.float32) * deviation
    if len(pieces) > 0:
        drawn = shard_levels(own_key, shape, pieces, -0.22, 0.18) * drawn
    return jnp.clip(drawn, min=-bound, max=bound).astype(held_as)


def heavy_noise(stream_key, shape, width, limit, cuts, heavy, kind=jnp.bfloat16):
    drawn = width * jax.random.normal(stream_key, shape, jnp.float32)
    if cuts:
        drawn = drawn * shard_levels(stream_key, shape, cuts, -0.22, 0.18)
    return jnp.clip(spiked(drawn, jax.random.fold_in(stream_key, 3), *heavy), -limit, limit).astype(kind)


def setup_inputs(seed: int = 0) -> dict:
    streams_of = jax.random.split(jax.random.key(seed), 10)
    rollout_q = draw_rollout_q(jax.random.fold_in(streams_of[9], 71), 0)
    rollout_k = draw_rollout_k(jax.random.fold_in(streams_of[9], 71), 0)
    rollout_value_rows = bell_draw(streams_of[2], (N_DP * SOURCE_ROWS, KEY_HEADS * HEAD_SIZE), 1.0, 6.0, ((0, 32), (1, 8)))
    q_gain = draw_q_gain(jax.random.fold_in(streams_of[9], 71), 0)
    k_gain = draw_k_gain(jax.random.fold_in(streams_of[9], 71), 0)
    out_weight = bell_draw(streams_of[5], (D, QUERY_HEADS * HEAD_SIZE), (QUERY_HEADS * HEAD_SIZE) ** -0.5, 0.09375, ((0, 32), (1, 8)))
    cotangent = heavy_noise(streams_of[6], (TOKENS, D), 1.0, 6.0, ((0, 32), (1, 8)), (0, 1, 32, 2.75))
    seq_lengths = draw_seq_lengths(jax.random.fold_in(streams_of[9], 71), 0)
    seq_source = draw_seq_source(jax.random.fold_in(streams_of[9], 71), 0)
    return dict(rollout_q=rollout_q, rollout_k=rollout_k, rollout_value_rows=rollout_value_rows, q_gain=q_gain, k_gain=k_gain, out_weight=out_weight, cotangent=cotangent, seq_lengths=seq_lengths, seq_source=seq_source)


NORM_EPS = 1e-06

def rms_norm(entries, gain):
    mean_sq = lax.optimization_barrier(jnp.mean(entries * entries, axis=-1, keepdims=True))
    return entries * lax.rsqrt(mean_sq + NORM_EPS) * gain

def weighted_values(form, left, right):
    return jnp.einsum(form, left.astype(jnp.float32), right.astype(jnp.float32))

def attend(q_rows, k_rows, v_rows, grad_rows, segment, position, q_gain, k_gain):
    row_sum_total = q_rows.shape[0]
    kv_heads = k_rows.shape[1] // HEAD_SIZE
    queries_per_group = q_rows.shape[1] // k_rows.shape[1]
    query_f32 = q_rows.astype(jnp.float32).reshape(row_sum_total, kv_heads, queries_per_group, HEAD_SIZE)
    key_f32 = k_rows.astype(jnp.float32).reshape(row_sum_total, kv_heads, HEAD_SIZE)
    normalized_queries = rms_norm(query_f32, q_gain).astype(jnp.bfloat16)
    normalized_keys = rms_norm(key_f32, k_gain).astype(jnp.bfloat16)
    value_rows = v_rows.reshape(row_sum_total, kv_heads, HEAD_SIZE)
    logit_scale = 1.0 / math.sqrt(HEAD_SIZE)
    allowed = (segment[:, None] == segment[None, :]) & (position[None, :] <= position[:, None])
    attention_logits = weighted_values('yepz,jez->epyj', normalized_queries, normalized_keys) * logit_scale
    attention_logits = jnp.where(allowed, attention_logits, -jnp.inf)
    row_max = lax.optimization_barrier(jnp.max(attention_logits, axis=-1, keepdims=True))
    exp_scores = jnp.exp(attention_logits - row_max)
    attn_probs = exp_scores / lax.optimization_barrier(jnp.sum(exp_scores, axis=-1, keepdims=True))
    probability_lower = attn_probs.astype(jnp.bfloat16)
    attention_lower = weighted_values('qecz,zqo->cqeo', probability_lower, value_rows).astype(jnp.bfloat16)
    output_gradient = grad_rows.reshape(row_sum_total, kv_heads, queries_per_group, HEAD_SIZE)
    packed_value_gradient = weighted_values('stnx,nstz->xsz', probability_lower, output_gradient).astype(jnp.bfloat16)
    probability_gradient = weighted_values('yepz,jez->epyj', output_gradient, value_rows)
    row_delta = lax.optimization_barrier(jnp.sum(attn_probs * probability_gradient, axis=-1, keepdims=True))
    score_gradient = (attn_probs * (probability_gradient - row_delta) * logit_scale).astype(jnp.bfloat16)
    normed_query_gradient = weighted_values('qecz,zqo->cqeo', score_gradient, normalized_keys)
    normed_key_gradient = weighted_values('stnx,nstz->xsz', score_gradient, normalized_queries)
    query_back = jax.vjp(lambda entries: rms_norm(entries, q_gain), query_f32)[1]
    key_back = jax.vjp(lambda entries: rms_norm(entries, k_gain), key_f32)[1]
    query_grad = query_back(normed_query_gradient)[0].astype(jnp.bfloat16)
    key_grad = key_back(normed_key_gradient)[0].astype(jnp.bfloat16)
    return (attention_lower.reshape(row_sum_total, -1), query_grad.reshape(row_sum_total, -1), key_grad.reshape(row_sum_total, -1), packed_value_gradient.reshape(row_sum_total, -1))

def reference(rollout_q, rollout_k, rollout_value_rows, q_gain, k_gain, out_weight, cotangent, seq_lengths, seq_source):
    lengths = seq_lengths.reshape(N_DP, SEQ_DEV)
    starts = (jnp.cumsum(lengths, axis=1) - lengths).astype(jnp.int32)
    seq_order = jnp.arange(NSEQ, dtype=jnp.int32)
    earlier = (seq_source[None, :] == seq_source[:, None]) & (seq_order[None, :] < seq_order[:, None])
    offsets = lax.optimization_barrier(jnp.sum(jnp.where(earlier, seq_lengths[None, :], 0), axis=1)).astype(jnp.int32)
    row_ids = jnp.arange(TOK_DEV, dtype=jnp.int32)
    inside = (row_ids[None, :, None] >= starts[:, None, :]).astype(jnp.int32)
    segment = (lax.optimization_barrier(jnp.sum(inside, axis=2)) - 1).astype(jnp.int32)
    seq_ids = (segment + SEQ_DEV * jnp.arange(N_DP, dtype=jnp.int32)[:, None]).astype(jnp.int32)
    position = (row_ids[None, :] - starts.reshape(-1)[seq_ids]).astype(jnp.int32)
    source_rows = (seq_source[seq_ids] * SOURCE_ROWS + offsets[seq_ids] + position).reshape(-1).astype(jnp.int32)
    packed_q = rollout_q[source_rows]
    packed_k = rollout_k[source_rows]
    packed_v = rollout_value_rows[source_rows]
    grad_attention = jnp.dot(cotangent, out_weight, preferred_element_type=jnp.float32).astype(jnp.bfloat16)

    def one_shard(items):
        return attend(items[0], items[1], items[2], items[3], items[4], items[5], q_gain, k_gain)
    per_shard = lax.map(one_shard, (packed_q.reshape(N_DP, TOK_DEV, -1), packed_k.reshape(N_DP, TOK_DEV, -1), packed_v.reshape(N_DP, TOK_DEV, -1), grad_attention.reshape(N_DP, TOK_DEV, -1), segment, position))
    attention = per_shard[0].reshape(TOKENS, -1)
    query_grad = per_shard[1].reshape(TOKENS, -1)
    key_grad = per_shard[2].reshape(TOKENS, -1)
    packed_value_gradient = per_shard[3].reshape(TOKENS, -1)
    group_cols = QUERY_HEADS * HEAD_SIZE // N_TENSOR

    def add_group(group_id, running):
        first_col = (group_id * group_cols).astype(jnp.int32)
        head_part = lax.dynamic_slice_in_dim(attention, first_col, group_cols, 1)
        weight_part = lax.dynamic_slice_in_dim(out_weight, first_col, group_cols, 1)
        term = jnp.dot(head_part, weight_part.T, preferred_element_type=jnp.float32)
        term = lax.optimization_barrier(term.astype(jnp.bfloat16))
        return running + term.astype(jnp.float32)
    layer_out = lax.fori_loop(0, N_TENSOR, add_group, jnp.zeros((TOKENS, D), jnp.float32)).astype(jnp.bfloat16)
    grad_scale = TOKENS ** (-0.5)

    def add_shard(shard_id, running):
        first_row = (shard_id * TOK_DEV).astype(jnp.int32)
        cot_rows = lax.dynamic_slice_in_dim(cotangent, first_row, TOK_DEV, 0)
        att_rows = lax.dynamic_slice_in_dim(attention, first_row, TOK_DEV, 0)
        term = jnp.dot(cot_rows.T, att_rows, preferred_element_type=jnp.float32) * grad_scale
        term = lax.optimization_barrier(term.astype(jnp.bfloat16))
        return running + term.astype(jnp.float32)
    weight_grad = lax.fori_loop(0, N_DP, add_shard, jnp.zeros((D, QUERY_HEADS * HEAD_SIZE), jnp.float32))
    return (layer_out, query_grad, key_grad, packed_value_gradient, weight_grad)
```

```python
import functools
import itertools
import math

import jax
import jax.numpy as jnp
from jax import lax
from jax.experimental import pallas as pl
from jax.experimental.pallas import tpu as pltpu
from jax.sharding import Mesh, PartitionSpec as P

EPS = 1e-06
BF = jnp.bfloat16
F32 = jnp.float32
ALL = ("z", "yl", "c", "yh", "x")
SIZES = (8, 2, 2, 2, 4)
TOK = 672
EDGE = 208
ROWS = 1064
BLK = 112
WIN = 384
NBLK = TOK // BLK
HEAD = 128
HEADS = 4
SCALE = 1.0 / math.sqrt(HEAD)
VMEM = 56 * 1024 * 1024


def params():
    return pltpu.CompilerParams(vmem_limit_bytes=VMEM)


def cost(flops, nbytes):
    return pl.CostEstimate(flops=int(flops), bytes_accessed=int(nbytes), transcendentals=0)


def window(i):
    return max(0, BLK * (i + 1) - WIN)


def dot(a, b, ca, cb):
    return lax.dot_general(a, b, (((ca,), (cb,)), ((), ())), preferred_element_type=F32)


def fwd_kernel(sc, rs, left, q, k, v, right, qg, kg, pk, p_out, o_out, com, qn, kn):
    com[0:EDGE, :] = left[...].astype(F32)
    com[EDGE : EDGE + ROWS, 0:512] = q[...].astype(F32)
    com[EDGE : EDGE + ROWS, 512:640] = k[...].astype(F32)
    com[EDGE : EDGE + ROWS, 640:768] = v[...].astype(F32)
    rest = lax.rem(sc[1], 8)
    at = pl.ds(pl.multiple_of(sc[1] - rest, 8), EDGE + 8)
    tail = jnp.concatenate([right[...].astype(F32), jnp.zeros((8, 768), F32)], axis=0)
    tail = pltpu.roll(tail, rest, 0)
    rows = lax.broadcasted_iota(jnp.int32, (EDGE + 8, 768), 0)
    com[at, :] = jnp.where(rows >= rest, tail, com[at, :])
    rest = lax.rem(sc[0], 8)
    base = pl.multiple_of(sc[0] - rest, 8)
    back = lax.rem(BLK + 8 - rest, BLK + 8)
    for i in range(NBLK):
        r = slice(BLK * i, BLK * (i + 1))
        x = com[pl.ds(base + BLK * i, BLK + 8), :]
        x = pltpu.roll(x, back, 0)[:BLK]
        pk[r, :] = x.astype(BF)
        for h in range(HEADS + 1):
            e = x[:, HEAD * h : HEAD * (h + 1)]
            ms = jnp.mean(e * e, axis=-1, keepdims=True)
            gain = qg[...] if h < HEADS else kg[...]
            n = (e * lax.rsqrt(ms + EPS) * gain).astype(BF)
            if h < HEADS:
                qn[r, HEAD * h : HEAD * (h + 1)] = n
            else:
                kn[r, :] = n
    for i in range(NBLK):
        r = slice(BLK * i, BLK * (i + 1))
        w = slice(window(i), window(i) + WIN)
        kw = kn[w, :]
        vw = pk[w, 640:768]
        qs = jnp.concatenate([qn[r, HEAD * h : HEAD * (h + 1)] for h in range(HEADS)], axis=0)
        s = dot(qs, kw, 1, 1)
        row = lax.broadcasted_iota(jnp.int32, (BLK, WIN), 0) + BLK * i
        col = lax.broadcasted_iota(jnp.int32, (BLK, WIN), 1) + window(i)
        ok = (col <= row) & (col >= rs[r, :])
        pbs = []
        for h in range(HEADS):
            sh = jnp.where(ok, s[BLK * h : BLK * (h + 1), :] * SCALE, -1e30)
            e = jnp.exp(sh - jnp.max(sh, axis=-1, keepdims=True))
            pr = e * (1.0 / jnp.sum(e, axis=-1, keepdims=True))
            p_out[i, BLK * h : BLK * (h + 1), :] = pr
            pbs.append(pr.astype(BF))
        o = dot(jnp.concatenate(pbs, axis=0), vw, 1, 0).astype(BF)
        for h in range(HEADS):
            o_out[r, HEAD * h : HEAD * (h + 1)] = o[BLK * h : BLK * (h + 1), :]


def forward(sc, rs, left, q, k, v, right, qg, kg):
    vm = pl.BlockSpec(memory_space=pltpu.VMEM)
    return pl.pallas_call(
        fwd_kernel,
        out_shape=(
            jax.ShapeDtypeStruct((TOK, 768), BF),
            jax.ShapeDtypeStruct((NBLK, HEADS * BLK, WIN), F32),
            jax.ShapeDtypeStruct((TOK, 512), BF),
        ),
        in_specs=[pl.BlockSpec(memory_space=pltpu.SMEM)] + [vm] * 8,
        out_specs=(vm, vm, vm),
        scratch_shapes=[
            pltpu.VMEM((EDGE + ROWS + EDGE + 8, 768), F32),
            pltpu.VMEM((TOK, 512), BF),
            pltpu.VMEM((TOK, HEAD), BF),
        ],
        compiler_params=params(),
        cost_estimate=cost(6e9, 9e6),
    )(sc, rs, left, q, k, v, right, qg, kg)


def norm_back(x, gain, dy):
    r = lax.rsqrt(jnp.mean(x * x, axis=-1, keepdims=True) + EPS)
    xh = x * r
    gd = gain * dy
    return r * (gd - xh * jnp.mean(xh * gd, axis=-1, keepdims=True))


def bwd_kernel(sel, gm, go, got, pk, p_in, qg, kg, dq, dk, dv, qn, kn, do, dk_acc, dv_acc):
    first = sel[0] == 1
    for i in range(NBLK):
        r = slice(BLK * i, BLK * (i + 1))
        for h in range(HEADS + 1):
            c = slice(HEAD * h, HEAD * (h + 1))
            e = pk[r, c].astype(F32)
            ms = jnp.mean(e * e, axis=-1, keepdims=True)
            gain = qg[...] if h < HEADS else kg[...]
            n = (e * lax.rsqrt(ms + EPS) * gain).astype(BF)
            if h < HEADS:
                qn[r, c] = n
                own = jnp.where(first, gm[r, c].astype(F32), go[r, c].astype(F32))
                do[r, c] = (own + got[r, c].astype(F32)).astype(BF)
            else:
                kn[r, :] = n
    dk_acc[...] = jnp.zeros_like(dk_acc)
    dv_acc[...] = jnp.zeros_like(dv_acc)
    for i in range(NBLK):
        r = slice(BLK * i, BLK * (i + 1))
        w = slice(window(i), window(i) + WIN)
        kw = kn[w, :]
        vw = pk[w, 640:768]
        qs = jnp.concatenate([qn[r, HEAD * h : HEAD * (h + 1)] for h in range(HEADS)], axis=0)
        ds_ = jnp.concatenate([do[r, HEAD * h : HEAD * (h + 1)] for h in range(HEADS)], axis=0)
        dp = dot(ds_, vw, 1, 1)
        dss, pbs = [], []
        for h in range(HEADS):
            rows = slice(BLK * h, BLK * (h + 1))
            pr = p_in[i, rows, :]
            dph = dp[rows, :]
            delta = jnp.sum(pr * dph, axis=-1, keepdims=True)
            dss.append((pr * (dph - delta) * SCALE).astype(BF))
            pbs.append(pr.astype(BF))
        dsc = jnp.concatenate(dss, axis=0)
        pb = jnp.concatenate(pbs, axis=0)
        dv_acc[w, :] += dot(pb, ds_, 0, 0)
        dk_acc[w, :] += dot(dsc, qs, 0, 0)
        dqn = dot(dsc, kw, 1, 0)
        for h in range(HEADS):
            c = slice(HEAD * h, HEAD * (h + 1))
            x = pk[r, c].astype(F32)
            dq[r, c] = norm_back(x, qg[...], dqn[BLK * h : BLK * (h + 1), :]).astype(BF)
    for i in range(NBLK):
        r = slice(BLK * i, BLK * (i + 1))
        dk[r, :] = norm_back(pk[r, 512:640].astype(F32), kg[...], dk_acc[r, :]).astype(BF)
        dv[r, :] = dv_acc[r, :].astype(BF)


def backward(sel, gm, go, got, pk, p, qg, kg):
    vm = pl.BlockSpec(memory_space=pltpu.VMEM)
    return pl.pallas_call(
        bwd_kernel,
        out_shape=(
            jax.ShapeDtypeStruct((TOK, 512), BF),
            jax.ShapeDtypeStruct((TOK, HEAD), BF),
            jax.ShapeDtypeStruct((TOK, HEAD), BF),
        ),
        in_specs=[pl.BlockSpec(memory_space=pltpu.SMEM)] + [vm] * 7,
        out_specs=(vm, vm, vm),
        scratch_shapes=[
            pltpu.VMEM((TOK, 512), BF),
            pltpu.VMEM((TOK, HEAD), BF),
            pltpu.VMEM((TOK, 512), BF),
            pltpu.VMEM((TOK, HEAD), F32),
            pltpu.VMEM((TOK, HEAD), F32),
        ],
        compiler_params=params(),
        cost_estimate=cost(6e9, 9e6),
    )(sel, gm, go, got, pk, p, qg, kg)


def halves_kernel(swap, rows, after, out0, out1):
    low, high = rows[0:160, :], rows[160:320, :]
    first = swap[0] == 0
    out0[...] = jnp.where(first, low, high)
    out1[...] = jnp.where(first, high, low)


def halves_of(swap, rows, after):
    vm = pl.BlockSpec(memory_space=pltpu.VMEM)
    out = jax.ShapeDtypeStruct((160, 512), BF)
    return pl.pallas_call(
        halves_kernel,
        out_shape=(out, out),
        in_specs=[
            pl.BlockSpec(memory_space=pltpu.SMEM),
            vm,
            pl.BlockSpec(memory_space=pl.ANY),
        ],
        out_specs=(vm, vm),
        compiler_params=params(),
        cost_estimate=cost(160 * 512, 1e6),
    )(swap, rows, after)


def product(a, b, ca, cb):
    return lax.dot_general(a, b, (((ca,), (cb,)), ((), ())), preferred_element_type=F32)


def shift(value, axis, k):
    n = lax.axis_size(axis)
    return lax.ppermute(value, axis, [(i, (i + k) % n) for i in range(n)])


def linear(z, yl, c, yh, x):
    return (((z * 2 + yl) * 2 + c) * 2 + yh) * 4 + x


def every(*sizes):
    return list(itertools.product(*(range(n) for n in sizes)))


def weight_moves(flip):
    return [
        (linear(4 * f + xh, r, s, h, x), linear(2 * (xh ^ (2 * h)) + r, s ^ flip, h, f, x))
        for f, xh, r, s, h, x in every(2, 4, 2, 2, 2, 4)
    ]


def final_moves(flip):
    return [
        (
            linear(4 * o + 2 * xl + r, s ^ flip, c, yh, x),
            linear(4 * yh + 2 * c + xl, r, s, yh ^ o, x),
        )
        for o, xl, r, s, c, yh, x in every(2, 2, 2, 2, 2, 2, 4)
    ]


def body(rollout_q, rollout_k, rollout_v, q_gain, k_gain, out_weight, cotangent, lengths, source):
    z, yl, c, yh, x = (lax.axis_index(name) for name in ALL)
    dp = (z * 2 + yl) * 2 + c
    shards = 32
    per = lengths.shape[0] // shards

    w_here, w_pair = (lax.ppermute(out_weight, ALL, weight_moves(flip)) for flip in (0, 1))
    w_both = jnp.where(
        yl == 0,
        jnp.concatenate([w_here, w_pair], axis=0),
        jnp.concatenate([w_pair, w_here], axis=0),
    )
    w_m = lax.all_gather(w_both, "z", axis=0, tiled=True)
    w_o = shift(w_m, "c", 1)

    total = jnp.sum(jnp.where(source == dp, lengths, 0))
    tail = total - EDGE
    to_right = jnp.concatenate(
        [lax.dynamic_slice_in_dim(a, tail, EDGE, 0) for a in (rollout_q, rollout_k, rollout_v)],
        axis=1,
    )
    to_left = jnp.concatenate([a[:EDGE] for a in (rollout_q, rollout_k, rollout_v)], axis=1)
    names = ("z", "yl", "c")
    left = lax.ppermute(to_right, names, [(i, i + 1) for i in range(shards - 1)])
    right = lax.ppermute(to_left, names, [(i, i - 1) for i in range(1, shards)])

    slots = [((x + k) % 4) ^ (2 * c) for k in range(4)]
    cots = jnp.zeros((TOK, 2560), BF)
    for k in (0, 1, 3, 2):
        part = shift(cotangent, "x", -k) if k else cotangent
        cots = lax.dynamic_update_slice(cots, part, (0, 640 * slots[k]))

    order = jnp.arange(lengths.shape[0], dtype=jnp.int32)
    first = dp * per
    mine_len = lax.dynamic_slice_in_dim(lengths, first, per)
    mine_src = lax.dynamic_slice_in_dim(source, first, per)
    ends = jnp.cumsum(mine_len)
    starts = ends - mine_len
    lead = jnp.sum(jnp.where(mine_src < dp, mine_len, 0))
    own_off = jnp.sum(jnp.where((source == dp) & (order < first), lengths, 0))
    row_ids = jnp.arange(TOK, dtype=jnp.int32)
    row_start = jnp.max(
        jnp.where(row_ids[:, None] >= starts[None, :], starts[None, :], 0), axis=1, keepdims=True
    )
    scalars = jnp.stack([EDGE + own_off - lead, EDGE + total]).astype(jnp.int32)
    qg = q_gain.reshape(1, HEAD)
    kg = k_gain.reshape(1, HEAD)
    packed, probs, att = forward(
        scalars, row_start, left, rollout_q, rollout_k, rollout_v, right, qg, kg
    )
    att_far = shift(att, "yh", 1)

    grad_scale = (TOK * shards) ** (-0.5)
    sums = []
    for rows in (att, att_far):
        send = (product(cots[:, 1280:], rows, 0, 0) * grad_scale).astype(BF)
        keep = (product(cots[:, :1280], rows, 0, 0) * grad_scale).astype(BF)
        got = shift(send, "c", 1)
        sums.append((keep.astype(F32) + got.astype(F32)).astype(BF))
    summed = lax.psum_scatter(
        jnp.concatenate(sums, axis=0), "z", scatter_dimension=0, tiled=True
    )

    same = yh == c
    part_m = product(cots, w_m, 1, 0).astype(BF)
    part_o = (
        product(cots[:, :1280], w_o[1280:], 1, 0) + product(cots[:, 1280:], w_o[:1280], 1, 0)
    ).astype(BF)
    got = shift(jnp.where(same, part_o, part_m), "yh", 1)
    query_grad, key_grad, value_grad = backward(
        same.astype(jnp.int32)[None], part_m, part_o, got, packed, probs, qg, kg
    )

    att_m = jnp.where(same, att, att_far)
    att_o = jnp.where(same, att_far, att)
    outs = {}
    for k in (2, 1, 3, 0):
        rows_m = lax.dynamic_slice_in_dim(w_m, 640 * slots[k], 640, 0)
        rows_o = lax.dynamic_slice_in_dim(w_o, 640 * (slots[k] ^ 2), 640, 0)
        outs[k] = (product(att_m, rows_m, 1, 1) + product(att_o, rows_o, 1, 1)).astype(BF)
    got = [shift(outs[k], "x", k).astype(F32) for k in (1, 2, 3)]
    layer_out = (outs[0].astype(F32) + got[0] + got[1] + got[2]).astype(BF)

    ready = halves_of(yl.astype(jnp.int32)[None], summed, key_grad)
    landed = [lax.ppermute(ready[flip], ALL, final_moves(flip)) for flip in (0, 1)]
    weight_grad = landed[0].astype(F32) + landed[1].astype(F32)
    return layer_out, query_grad, key_grad, value_grad, weight_grad


def solution(mesh):
    grid = Mesh(mesh.devices.reshape(SIZES), ALL)
    dp, tensor = ("z", "yl", "c"), ("yh", "x")
    two = P(dp, tensor)
    return jax.shard_map(
        body,
        mesh=grid,
        in_specs=(two, two, two, P(), P(), two, two, P(), P()),
        out_specs=(two,) * 5,
        check_vma=False,
    )
```

```python
import functools
import itertools
import math

import jax
import jax.numpy as jnp
from jax import lax
from jax.experimental import pallas as pl
from jax.experimental.pallas import tpu as pltpu
from jax.sharding import Mesh, PartitionSpec as P

EPS = 1e-06
BF = jnp.bfloat16
F32 = jnp.float32
ALL = ("z", "yl", "c", "yh", "x")
SIZES = (8, 2, 2, 2, 4)
TOK = 672
EDGE = 208
ROWS = 1064
BLK = 112
WIN = 384
NBLK = TOK // BLK
HEAD = 128
HEADS = 4
SCALE = 1.0 / math.sqrt(HEAD)
VMEM = 56 * 1024 * 1024


def params():
    return pltpu.CompilerParams(vmem_limit_bytes=VMEM)


def cost(flops, nbytes):
    return pl.CostEstimate(flops=int(flops), bytes_accessed=int(nbytes), transcendentals=0)


def window(i):
    return max(0, BLK * (i + 1) - WIN)


def dot(a, b, ca, cb):
    return lax.dot_general(a, b, (((ca,), (cb,)), ((), ())), preferred_element_type=F32)


def fwd_kernel(sc, rs, left, q, k, v, right, qg, kg, pk, p_out, o_out, com, qn, kn):
    com[0:EDGE, :] = left[...].astype(F32)
    com[EDGE : EDGE + ROWS, 0:512] = q[...].astype(F32)
    com[EDGE : EDGE + ROWS, 512:640] = k[...].astype(F32)
    com[EDGE : EDGE + ROWS, 640:768] = v[...].astype(F32)
    rest = lax.rem(sc[1], 8)
    at = pl.ds(pl.multiple_of(sc[1] - rest, 8), EDGE + 8)
    tail = jnp.concatenate([right[...].astype(F32), jnp.zeros((8, 768), F32)], axis=0)
    tail = pltpu.roll(tail, rest, 0)
    rows = lax.broadcasted_iota(jnp.int32, (EDGE + 8, 768), 0)
    com[at, :] = jnp.where(rows >= rest, tail, com[at, :])
    rest = lax.rem(sc[0], 8)
    base = pl.multiple_of(sc[0] - rest, 8)
    back = lax.rem(BLK + 8 - rest, BLK + 8)
    for i in range(NBLK):
        r = slice(BLK * i, BLK * (i + 1))
        x = com[pl.ds(base + BLK * i, BLK + 8), :]
        x = pltpu.roll(x, back, 0)[:BLK]
        pk[r, :] = x.astype(BF)
        for h in range(HEADS + 1):
            e = x[:, HEAD * h : HEAD * (h + 1)]
            ms = jnp.mean(e * e, axis=-1, keepdims=True)
            gain = qg[...] if h < HEADS else kg[...]
            n = (e * lax.rsqrt(ms + EPS) * gain).astype(BF)
            if h < HEADS:
                qn[r, HEAD * h : HEAD * (h + 1)] = n
            else:
                kn[r, :] = n
    for i in range(NBLK):
        r = slice(BLK * i, BLK * (i + 1))
        w = slice(window(i), window(i) + WIN)
        kw = kn[w, :]
        vw = pk[w, 640:768]
        qs = jnp.concatenate([qn[r, HEAD * h : HEAD * (h + 1)] for h in range(HEADS)], axis=0)
        s = dot(qs, kw, 1, 1)
        row = lax.broadcasted_iota(jnp.int32, (BLK, WIN), 0) + BLK * i
        col = lax.broadcasted_iota(jnp.int32, (BLK, WIN), 1) + window(i)
        ok = (col <= row) & (col >= rs[r, :])
        pbs = []
        for h in range(HEADS):
            sh = jnp.where(ok, s[BLK * h : BLK * (h + 1), :] * SCALE, -1e30)
            e = jnp.exp(sh - jnp.max(sh, axis=-1, keepdims=True))
            pr = e * (1.0 / jnp.sum(e, axis=-1, keepdims=True))
            p_out[i, BLK * h : BLK * (h + 1), :] = pr
            pbs.append(pr.astype(BF))
        o = dot(jnp.concatenate(pbs, axis=0), vw, 1, 0).astype(BF)
        for h in range(HEADS):
            o_out[r, HEAD * h : HEAD * (h + 1)] = o[BLK * h : BLK * (h + 1), :]


def forward(sc, rs, left, q, k, v, right, qg, kg):
    vm = pl.BlockSpec(memory_space=pltpu.VMEM)
    return pl.pallas_call(
        fwd_kernel,
        out_shape=(
            jax.ShapeDtypeStruct((TOK, 768), BF),
            jax.ShapeDtypeStruct((NBLK, HEADS * BLK, WIN), F32),
            jax.ShapeDtypeStruct((TOK, 512), BF),
        ),
        in_specs=[pl.BlockSpec(memory_space=pltpu.SMEM)] + [vm] * 8,
        out_specs=(vm, vm, vm),
        scratch_shapes=[
            pltpu.VMEM((EDGE + ROWS + EDGE + 8, 768), F32),
            pltpu.VMEM((TOK, 512), BF),
            pltpu.VMEM((TOK, HEAD), BF),
        ],
        compiler_params=params(),
        cost_estimate=cost(3e10, 9e6),
    )(sc, rs, left, q, k, v, right, qg, kg)


def norm_back(x, gain, dy):
    r = lax.rsqrt(jnp.mean(x * x, axis=-1, keepdims=True) + EPS)
    xh = x * r
    gd = gain * dy
    return r * (gd - xh * jnp.mean(xh * gd, axis=-1, keepdims=True))


def bwd_kernel(sel, gm, go, got, pk, p_in, qg, kg, dq, dk, dv, qn, kn, do, dk_acc, dv_acc):
    first = sel[0] == 1
    for i in range(NBLK):
        r = slice(BLK * i, BLK * (i + 1))
        for h in range(HEADS + 1):
            c = slice(HEAD * h, HEAD * (h + 1))
            e = pk[r, c].astype(F32)
            ms = jnp.mean(e * e, axis=-1, keepdims=True)
            gain = qg[...] if h < HEADS else kg[...]
            n = (e * lax.rsqrt(ms + EPS) * gain).astype(BF)
            if h < HEADS:
                qn[r, c] = n
                own = jnp.where(first, gm[r, c].astype(F32), go[r, c].astype(F32))
                do[r, c] = (own + got[r, c].astype(F32)).astype(BF)
            else:
                kn[r, :] = n
    dk_acc[...] = jnp.zeros_like(dk_acc)
    dv_acc[...] = jnp.zeros_like(dv_acc)
    for i in range(NBLK):
        r = slice(BLK * i, BLK * (i + 1))
        w = slice(window(i), window(i) + WIN)
        kw = kn[w, :]
        vw = pk[w, 640:768]
        qs = jnp.concatenate([qn[r, HEAD * h : HEAD * (h + 1)] for h in range(HEADS)], axis=0)
        ds_ = jnp.concatenate([do[r, HEAD * h : HEAD * (h + 1)] for h in range(HEADS)], axis=0)
        dp = dot(ds_, vw, 1, 1)
        dss, pbs = [], []
        for h in range(HEADS):
            rows = slice(BLK * h, BLK * (h + 1))
            pr = p_in[i, rows, :]
            dph = dp[rows, :]
            delta = jnp.sum(pr * dph, axis=-1, keepdims=True)
            dss.append((pr * (dph - delta) * SCALE).astype(BF))
            pbs.append(pr.astype(BF))
        dsc = jnp.concatenate(dss, axis=0)
        pb = jnp.concatenate(pbs, axis=0)
        dv_acc[w, :] += dot(pb, ds_, 0, 0)
        dk_acc[w, :] += dot(dsc, qs, 0, 0)
        dqn = dot(dsc, kw, 1, 0)
        for h in range(HEADS):
            c = slice(HEAD * h, HEAD * (h + 1))
            x = pk[r, c].astype(F32)
            dq[r, c] = norm_back(x, qg[...], dqn[BLK * h : BLK * (h + 1), :]).astype(BF)
    for i in range(NBLK):
        r = slice(BLK * i, BLK * (i + 1))
        dk[r, :] = norm_back(pk[r, 512:640].astype(F32), kg[...], dk_acc[r, :]).astype(BF)
        dv[r, :] = dv_acc[r, :].astype(BF)


def backward(sel, gm, go, got, pk, p, qg, kg):
    vm = pl.BlockSpec(memory_space=pltpu.VMEM)
    return pl.pallas_call(
        bwd_kernel,
        out_shape=(
            jax.ShapeDtypeStruct((TOK, 512), BF),
            jax.ShapeDtypeStruct((TOK, HEAD), BF),
            jax.ShapeDtypeStruct((TOK, HEAD), BF),
        ),
        in_specs=[pl.BlockSpec(memory_space=pltpu.SMEM)] + [vm] * 7,
        out_specs=(vm, vm, vm),
        scratch_shapes=[
            pltpu.VMEM((TOK, 512), BF),
            pltpu.VMEM((TOK, HEAD), BF),
            pltpu.VMEM((TOK, 512), BF),
            pltpu.VMEM((TOK, HEAD), F32),
            pltpu.VMEM((TOK, HEAD), F32),
        ],
        compiler_params=params(),
        cost_estimate=cost(6e9, 9e6),
    )(sel, gm, go, got, pk, p, qg, kg)


def halves_kernel(swap, rows, after, out0, out1):
    low, high = rows[0:160, :], rows[160:320, :]
    first = swap[0] == 0
    out0[...] = jnp.where(first, low, high)
    out1[...] = jnp.where(first, high, low)


def halves_of(swap, rows, after):
    vm = pl.BlockSpec(memory_space=pltpu.VMEM)
    out = jax.ShapeDtypeStruct((160, 512), BF)
    return pl.pallas_call(
        halves_kernel,
        out_shape=(out, out),
        in_specs=[
            pl.BlockSpec(memory_space=pltpu.SMEM),
            vm,
            pl.BlockSpec(memory_space=pl.ANY),
        ],
        out_specs=(vm, vm),
        compiler_params=params(),
        cost_estimate=cost(160 * 512, 1e6),
    )(swap, rows, after)


def pair_kernel(swap, here, pair, out):
    first = swap[0] == 0
    out[0:160, :] = jnp.where(first, here[...], pair[...])
    out[160:320, :] = jnp.where(first, pair[...], here[...])


def pair_of(swap, here, pair):
    vm = pl.BlockSpec(memory_space=pltpu.VMEM)
    return pl.pallas_call(
        pair_kernel,
        out_shape=jax.ShapeDtypeStruct((320, 512), BF),
        in_specs=[pl.BlockSpec(memory_space=pltpu.SMEM), vm, vm],
        out_specs=vm,
        compiler_params=params(),
        cost_estimate=cost(1, 1),
    )(swap, here, pair)


def hold_kernel(*refs):
    pass


def hold(value, *after):
    return pl.pallas_call(
        hold_kernel,
        out_shape=jax.ShapeDtypeStruct(value.shape, value.dtype),
        in_specs=[pl.BlockSpec(memory_space=pl.ANY)] * (1 + len(after)),
        out_specs=pl.BlockSpec(memory_space=pl.ANY),
        input_output_aliases={0: 0},
        cost_estimate=cost(1, 1),
    )(value, *after)


def product(a, b, ca, cb):
    return lax.dot_general(a, b, (((ca,), (cb,)), ((), ())), preferred_element_type=F32)


def shift(value, axis, k):
    n = lax.axis_size(axis)
    return lax.ppermute(value, axis, [(i, (i + k) % n) for i in range(n)])


def linear(z, yl, c, yh, x):
    return (((z * 2 + yl) * 2 + c) * 2 + yh) * 4 + x


def every(*sizes):
    return list(itertools.product(*(range(n) for n in sizes)))


def place(xh, f):
    high = xh // 2
    return (2 * ((xh + high + f + 1) % 2)) + 1 - high


def weight_moves():
    return [
        (linear(4 * f + xh, r, c, h, x), linear(2 * place(xh, f) + r, c, h, f, x))
        for f, xh, r, c, h, x in every(2, 4, 2, 2, 2, 4)
    ]


def final_moves(flip):
    moves = []
    for o, r, s, yh, x, xh in every(2, 2, 2, 2, 4, 4):
        c, low = divmod(place(xh, yh), 2)
        moves.append(
            (
                linear(4 * o + 2 * low + r, s ^ flip, c, yh, x),
                linear(4 * yh + xh, r, s, yh ^ o, x),
            )
        )
    return moves


def body(rollout_q, rollout_k, rollout_v, q_gain, k_gain, out_weight, cotangent, lengths, source):
    z, yl, c, yh, x = (lax.axis_index(name) for name in ALL)
    dp = (z * 2 + yl) * 2 + c
    shards = 32
    per = lengths.shape[0] // shards

    core = c.astype(jnp.int32)[None]
    w_chip = pair_of(core, out_weight, shift(out_weight, "c", 1))

    lengths, source = hold(lengths, w_chip), hold(source, w_chip)

    total = jnp.sum(jnp.where(source == dp, lengths, 0))
    tail = total - EDGE
    to_right = jnp.concatenate(
        [lax.dynamic_slice_in_dim(a, tail, EDGE, 0) for a in (rollout_q, rollout_k, rollout_v)],
        axis=1,
    )
    to_left = jnp.concatenate([a[:EDGE] for a in (rollout_q, rollout_k, rollout_v)], axis=1)

    w_moved = lax.ppermute(w_chip, ALL, weight_moves())

    names = ("z", "yl", "c")
    to_left = hold(to_left, w_chip)
    left = lax.ppermute(to_right, names, [(i, i + 1) for i in range(shards - 1)])
    right = lax.ppermute(to_left, names, [(i, i - 1) for i in range(1, shards)])

    slots = [place((x + k) % 4, yh) for k in range(4)]
    cots = jnp.zeros((TOK, 2560), BF)
    for k in (0, 1, 3, 2):
        part = shift(cotangent, "x", -k) if k else cotangent
        cots = lax.dynamic_update_slice(cots, part, (0, 640 * slots[k]))

    order = jnp.arange(lengths.shape[0], dtype=jnp.int32)
    first = dp * per
    mine_len = lax.dynamic_slice_in_dim(lengths, first, per)
    mine_src = lax.dynamic_slice_in_dim(source, first, per)
    ends = jnp.cumsum(mine_len)
    starts = ends - mine_len
    lead = jnp.sum(jnp.where(mine_src < dp, mine_len, 0))
    own_off = jnp.sum(jnp.where((source == dp) & (order < first), lengths, 0))
    row_ids = jnp.arange(TOK, dtype=jnp.int32)
    row_start = jnp.max(
        jnp.where(row_ids[:, None] >= starts[None, :], starts[None, :], 0), axis=1, keepdims=True
    )
    scalars = jnp.stack([EDGE + own_off - lead, EDGE + total]).astype(jnp.int32)
    qg = q_gain.reshape(1, HEAD)
    kg = k_gain.reshape(1, HEAD)
    packed, probs, att = forward(
        scalars, row_start, left, rollout_q, rollout_k, rollout_v, right, qg, kg
    )
    att_far = shift(att, "yh", 1)

    w_m = lax.all_gather(w_moved, "z", axis=0, tiled=True)
    w_o = shift(w_m, "c", 1)

    grad_scale = (TOK * shards) ** (-0.5)
    cots_send = lax.dynamic_slice_in_dim(cots, 1280 * (1 - c), 1280, 1)
    cots_keep = lax.dynamic_slice_in_dim(cots, 1280 * c, 1280, 1)

    def half(columns, rows):
        return (product(columns, rows, 0, 0) * grad_scale).astype(BF)

    both = jnp.concatenate([att, att_far], axis=1)
    got = shift(half(cots_send, both), "c", 1)
    keep = half(cots_keep, hold(both, w_m))
    sums = (keep.astype(F32) + got.astype(F32)).astype(BF)
    sums = jnp.concatenate([sums[:, :512], sums[:, 512:]], axis=0)
    summed = lax.psum_scatter(sums, "z", scatter_dimension=0, tiled=True)

    same = yh == c
    part_m = product(cots, w_m, 1, 0).astype(BF)
    part_o = product(cots, w_o, 1, 0).astype(BF)
    got = shift(jnp.where(same, part_o, part_m), "yh", 1)
    query_grad, key_grad, value_grad = backward(
        same.astype(jnp.int32)[None], part_m, part_o, got, packed, probs, qg, kg
    )

    att_m = jnp.where(same, att, att_far)
    att_o = jnp.where(same, att_far, att)
    outs = {}
    for k in (2, 1, 3, 0):
        rows_m = lax.dynamic_slice_in_dim(w_m, 640 * slots[k], 640, 0)
        rows_o = lax.dynamic_slice_in_dim(w_o, 640 * slots[k], 640, 0)
        outs[k] = (product(att_m, rows_m, 1, 1) + product(att_o, rows_o, 1, 1)).astype(BF)
    got = [shift(outs[k], "x", k).astype(F32) for k in (1, 2, 3)]
    layer_out = (outs[0].astype(F32) + got[0] + got[1] + got[2]).astype(BF)

    ready = halves_of(yl.astype(jnp.int32)[None], summed, key_grad)
    landed = [lax.ppermute(ready[flip], ALL, final_moves(flip)) for flip in (0, 1)]
    weight_grad = landed[0].astype(F32) + landed[1].astype(F32)
    return layer_out, query_grad, key_grad, value_grad, weight_grad


def solution(mesh):
    grid = Mesh(mesh.devices.reshape(SIZES), ALL)
    dp, tensor = ("z", "yl", "c"), ("yh", "x")
    two = P(dp, tensor)
    return jax.shard_map(
        body,
        mesh=grid,
        in_specs=(two, two, two, P(), P(), two, two, P(), P()),
        out_specs=(two,) * 5,
        check_vma=False,
    )
```

```python
import functools
import itertools
import math

import jax
import jax.numpy as jnp
from jax import lax
from jax.experimental import pallas as pl
from jax.experimental.pallas import tpu as pltpu
from jax.sharding import Mesh, PartitionSpec as P

EPS = 1e-06
BF = jnp.bfloat16
F32 = jnp.float32
ALL = ("z", "yl", "c", "yh", "x")
SIZES = (8, 2, 2, 2, 4)
TOK = 672
EDGE = 208
ROWS = 1064
BLK = 112
WIN = 384
NBLK = TOK // BLK
SEQS = 6
HEAD = 128
HEADS = 4
SCALE = 1.0 / math.sqrt(HEAD)
VMEM = 56 * 1024 * 1024


def params():
    return pltpu.CompilerParams(vmem_limit_bytes=VMEM)


def cost(flops, nbytes):
    return pl.CostEstimate(flops=int(flops), bytes_accessed=int(nbytes), transcendentals=0)


def window(i):
    return max(0, BLK * (i + 1) - WIN)


def dot(a, b, ca, cb):
    return lax.dot_general(a, b, (((ca,), (cb,)), ((), ())), preferred_element_type=F32)


def edge_kernel(place, lengths, source, q, k, v, after, to_right, to_left, sc, wide):
    me = place[0]
    first = SEQS * me
    count = lengths.shape[0]

    def held(i):
        j = jnp.clip(i, 0, count - 1)
        return jnp.where((i == j) & (source[j] == me), lengths[j], 0)

    before = held(first - 1)
    total = before
    for t in range(SEQS + 1):
        total = total + held(first + t)
    lead = jnp.where(source[first] < me, lengths[first], 0)
    sc[0] = EDGE + before - lead
    sc[1] = EDGE + total
    begin = jnp.int32(0)
    for t in range(SEQS):
        sc[2 + t] = begin
        begin = begin + lengths[first + t]

    wide[0:ROWS, 0:512] = q[...].astype(F32)
    wide[0:ROWS, 512:640] = k[...].astype(F32)
    wide[0:ROWS, 640:768] = v[...].astype(F32)
    tail = jnp.clip(total - EDGE, 0, ROWS - EDGE)
    rest = lax.rem(tail, 8)
    rows = wide[pl.ds(pl.multiple_of(tail - rest, 8), EDGE + 8), :]
    rows = pltpu.roll(rows, lax.rem(EDGE + 8 - rest, EDGE + 8), 0)
    to_right[...] = rows[:EDGE].astype(BF)
    to_left[:, 0:512] = q[0:EDGE, :]
    to_left[:, 512:640] = k[0:EDGE, :]
    to_left[:, 640:768] = v[0:EDGE, :]


def edges(place, lengths, source, q, k, v, after):
    vm = pl.BlockSpec(memory_space=pltpu.VMEM)
    sm = pl.BlockSpec(memory_space=pltpu.SMEM)
    out = jax.ShapeDtypeStruct((EDGE, 768), BF)
    return pl.pallas_call(
        edge_kernel,
        out_shape=(out, out, jax.ShapeDtypeStruct((2 + SEQS,), jnp.int32)),
        in_specs=[sm, sm, sm, vm, vm, vm, pl.BlockSpec(memory_space=pl.ANY)],
        out_specs=(vm, vm, sm),
        scratch_shapes=[pltpu.VMEM((ROWS + 8, 768), F32)],
        compiler_params=params(),
        cost_estimate=cost(1, 1),
    )(place, lengths, source, q, k, v, after)


def fwd_kernel(sc, left, q, k, v, right, qg, kg, pk, p_out, o_out, com, qn, kn, p_buf, sems):
    com[0:EDGE, :] = left[...].astype(F32)
    com[EDGE : EDGE + ROWS, 0:512] = q[...].astype(F32)
    com[EDGE : EDGE + ROWS, 512:640] = k[...].astype(F32)
    com[EDGE : EDGE + ROWS, 640:768] = v[...].astype(F32)
    rest = lax.rem(sc[1], 8)
    at = pl.ds(pl.multiple_of(sc[1] - rest, 8), EDGE + 8)
    tail = jnp.concatenate([right[...].astype(F32), jnp.zeros((8, 768), F32)], axis=0)
    tail = pltpu.roll(tail, rest, 0)
    rows = lax.broadcasted_iota(jnp.int32, (EDGE + 8, 768), 0)
    com[at, :] = jnp.where(rows >= rest, tail, com[at, :])
    rest = lax.rem(sc[0], 8)
    base = pl.multiple_of(sc[0] - rest, 8)
    back = lax.rem(BLK + 8 - rest, BLK + 8)
    for i in range(NBLK):
        r = slice(BLK * i, BLK * (i + 1))
        x = com[pl.ds(base + BLK * i, BLK + 8), :]
        x = pltpu.roll(x, back, 0)[:BLK]
        pk[r, :] = x.astype(BF)
        for h in range(HEADS + 1):
            e = x[:, HEAD * h : HEAD * (h + 1)]
            ms = jnp.mean(e * e, axis=-1, keepdims=True)
            gain = qg[...] if h < HEADS else kg[...]
            n = (e * lax.rsqrt(ms + EPS) * gain).astype(BF)
            if h < HEADS:
                qn[r, HEAD * h : HEAD * (h + 1)] = n
            else:
                kn[r, :] = n
    for i in range(NBLK):
        r = slice(BLK * i, BLK * (i + 1))
        w = slice(window(i), window(i) + WIN)
        kw = kn[w, :]
        vw = pk[w, 640:768]
        qs = jnp.concatenate([qn[r, HEAD * h : HEAD * (h + 1)] for h in range(HEADS)], axis=0)
        s = dot(qs, kw, 1, 1)
        row = lax.broadcasted_iota(jnp.int32, (BLK, WIN), 0) + BLK * i
        col = lax.broadcasted_iota(jnp.int32, (BLK, WIN), 1) + window(i)
        line = lax.broadcasted_iota(jnp.int32, (BLK, 1), 0) + BLK * i
        begin = jnp.zeros((BLK, 1), jnp.int32)
        for j in range(1, SEQS):
            begin = jnp.where(line >= sc[2 + j], sc[2 + j], begin)
        ok = (col <= row) & (col >= begin)
        pbs = []
        for h in range(HEADS):
            sh = jnp.where(ok, s[BLK * h : BLK * (h + 1), :] * SCALE, -1e30)
            e = jnp.exp(sh - jnp.max(sh, axis=-1, keepdims=True))
            pr = e * (1.0 / jnp.sum(e, axis=-1, keepdims=True))
            p_buf[i, BLK * h : BLK * (h + 1), :] = pr
            pbs.append(pr.astype(BF))
        pltpu.make_async_copy(p_buf.at[i], p_out.at[i], sems.at[i]).start()
        o = dot(jnp.concatenate(pbs, axis=0), vw, 1, 0).astype(BF)
        for h in range(HEADS):
            o_out[r, HEAD * h : HEAD * (h + 1)] = o[BLK * h : BLK * (h + 1), :]
    for i in range(NBLK):
        pltpu.make_async_copy(p_buf.at[i], p_out.at[i], sems.at[i]).wait()


def forward(sc, left, q, k, v, right, qg, kg):
    vm = pl.BlockSpec(memory_space=pltpu.VMEM)
    return pl.pallas_call(
        fwd_kernel,
        out_shape=(
            jax.ShapeDtypeStruct((TOK, 768), BF),
            jax.ShapeDtypeStruct((NBLK, HEADS * BLK, WIN), F32),
            jax.ShapeDtypeStruct((TOK, 512), BF),
        ),
        in_specs=[pl.BlockSpec(memory_space=pltpu.SMEM)] + [vm] * 7,
        out_specs=(vm, pl.BlockSpec(memory_space=pl.ANY), vm),
        scratch_shapes=[
            pltpu.VMEM((EDGE + ROWS + EDGE + 8, 768), F32),
            pltpu.VMEM((TOK, 512), BF),
            pltpu.VMEM((TOK, HEAD), BF),
            pltpu.VMEM((NBLK, HEADS * BLK, WIN), F32),
            pltpu.SemaphoreType.DMA((NBLK,)),
        ],
        compiler_params=params(),
        cost_estimate=cost(3e10, 9e6),
    )(sc, left, q, k, v, right, qg, kg)


def norm_back(x, gain, dy):
    r = lax.rsqrt(jnp.mean(x * x, axis=-1, keepdims=True) + EPS)
    xh = x * r
    gd = gain * dy
    return r * (gd - xh * jnp.mean(xh * gd, axis=-1, keepdims=True))


def bwd_kernel(
    sel, gm, go, got, pk, p_in, qg, kg, dq, dk, dv, qn, kn, do, dk_acc, dv_acc, p_buf, sems
):
    for i in range(NBLK):
        pltpu.make_async_copy(p_in.at[i], p_buf.at[i], sems.at[i]).start()
    first = sel[0] == 1
    for i in range(NBLK):
        r = slice(BLK * i, BLK * (i + 1))
        for h in range(HEADS + 1):
            c = slice(HEAD * h, HEAD * (h + 1))
            e = pk[r, c].astype(F32)
            ms = jnp.mean(e * e, axis=-1, keepdims=True)
            gain = qg[...] if h < HEADS else kg[...]
            n = (e * lax.rsqrt(ms + EPS) * gain).astype(BF)
            if h < HEADS:
                qn[r, c] = n
                own = jnp.where(first, gm[r, c].astype(F32), go[r, c].astype(F32))
                do[r, c] = (own + got[r, c].astype(F32)).astype(BF)
            else:
                kn[r, :] = n
    dk_acc[...] = jnp.zeros_like(dk_acc)
    dv_acc[...] = jnp.zeros_like(dv_acc)
    for i in range(NBLK):
        r = slice(BLK * i, BLK * (i + 1))
        w = slice(window(i), window(i) + WIN)
        kw = kn[w, :]
        vw = pk[w, 640:768]
        qs = jnp.concatenate([qn[r, HEAD * h : HEAD * (h + 1)] for h in range(HEADS)], axis=0)
        ds_ = jnp.concatenate([do[r, HEAD * h : HEAD * (h + 1)] for h in range(HEADS)], axis=0)
        dp = dot(ds_, vw, 1, 1)
        pltpu.make_async_copy(p_in.at[i], p_buf.at[i], sems.at[i]).wait()
        dss, pbs = [], []
        for h in range(HEADS):
            rows = slice(BLK * h, BLK * (h + 1))
            pr = p_buf[i, rows, :]
            dph = dp[rows, :]
            delta = jnp.sum(pr * dph, axis=-1, keepdims=True)
            dss.append((pr * (dph - delta) * SCALE).astype(BF))
            pbs.append(pr.astype(BF))
        dsc = jnp.concatenate(dss, axis=0)
        pb = jnp.concatenate(pbs, axis=0)
        dv_acc[w, :] += dot(pb, ds_, 0, 0)
        dk_acc[w, :] += dot(dsc, qs, 0, 0)
        dqn = dot(dsc, kw, 1, 0)
        for h in range(HEADS):
            c = slice(HEAD * h, HEAD * (h + 1))
            x = pk[r, c].astype(F32)
            dq[r, c] = norm_back(x, qg[...], dqn[BLK * h : BLK * (h + 1), :]).astype(BF)
    for i in range(NBLK):
        r = slice(BLK * i, BLK * (i + 1))
        dk[r, :] = norm_back(pk[r, 512:640].astype(F32), kg[...], dk_acc[r, :]).astype(BF)
        dv[r, :] = dv_acc[r, :].astype(BF)


def backward(sel, gm, go, got, pk, p, qg, kg):
    vm = pl.BlockSpec(memory_space=pltpu.VMEM)
    return pl.pallas_call(
        bwd_kernel,
        out_shape=(
            jax.ShapeDtypeStruct((TOK, 512), BF),
            jax.ShapeDtypeStruct((TOK, HEAD), BF),
            jax.ShapeDtypeStruct((TOK, HEAD), BF),
        ),
        in_specs=[pl.BlockSpec(memory_space=pltpu.SMEM)]
        + [vm] * 4
        + [pl.BlockSpec(memory_space=pl.ANY), vm, vm],
        out_specs=(vm, vm, vm),
        scratch_shapes=[
            pltpu.VMEM((TOK, 512), BF),
            pltpu.VMEM((TOK, HEAD), BF),
            pltpu.VMEM((TOK, 512), BF),
            pltpu.VMEM((TOK, HEAD), F32),
            pltpu.VMEM((TOK, HEAD), F32),
            pltpu.VMEM((NBLK, HEADS * BLK, WIN), F32),
            pltpu.SemaphoreType.DMA((NBLK,)),
        ],
        compiler_params=params(),
        cost_estimate=cost(6e9, 9e6),
    )(sel, gm, go, got, pk, p, qg, kg)


def halves_kernel(swap, rows, after, out0, out1):
    low, high = rows[0:160, :], rows[160:320, :]
    first = swap[0] == 0
    out0[...] = jnp.where(first, low, high)
    out1[...] = jnp.where(first, high, low)


def halves_of(swap, rows, after):
    vm = pl.BlockSpec(memory_space=pltpu.VMEM)
    out = jax.ShapeDtypeStruct((160, 512), BF)
    return pl.pallas_call(
        halves_kernel,
        out_shape=(out, out),
        in_specs=[
            pl.BlockSpec(memory_space=pltpu.SMEM),
            vm,
            pl.BlockSpec(memory_space=pl.ANY),
        ],
        out_specs=(vm, vm),
        compiler_params=params(),
        cost_estimate=cost(160 * 512, 1e6),
    )(swap, rows, after)


def pair_kernel(swap, here, pair, out):
    first = swap[0] == 0
    out[0:160, :] = jnp.where(first, here[...], pair[...])
    out[160:320, :] = jnp.where(first, pair[...], here[...])


def pair_of(swap, here, pair):
    vm = pl.BlockSpec(memory_space=pltpu.VMEM)
    return pl.pallas_call(
        pair_kernel,
        out_shape=jax.ShapeDtypeStruct((320, 512), BF),
        in_specs=[pl.BlockSpec(memory_space=pltpu.SMEM), vm, vm],
        out_specs=vm,
        compiler_params=params(),
        cost_estimate=cost(1, 1),
    )(swap, here, pair)


def hold_kernel(*refs):
    pass


def hold(value, *after):
    return pl.pallas_call(
        hold_kernel,
        out_shape=jax.ShapeDtypeStruct(value.shape, value.dtype),
        in_specs=[pl.BlockSpec(memory_space=pl.ANY)] * (1 + len(after)),
        out_specs=pl.BlockSpec(memory_space=pl.ANY),
        input_output_aliases={0: 0},
        cost_estimate=cost(1, 1),
    )(value, *after)


def product(a, b, ca, cb):
    return lax.dot_general(a, b, (((ca,), (cb,)), ((), ())), preferred_element_type=F32)


def shift(value, axis, k):
    n = lax.axis_size(axis)
    return lax.ppermute(value, axis, [(i, (i + k) % n) for i in range(n)])


def linear(z, yl, c, yh, x):
    return (((z * 2 + yl) * 2 + c) * 2 + yh) * 4 + x


def every(*sizes):
    return list(itertools.product(*(range(n) for n in sizes)))


def place(xh, f):
    high = xh // 2
    return (2 * ((xh + high + f + 1) % 2)) + 1 - high


def weight_moves():
    return [
        (linear(4 * f + xh, r, c, h, x), linear(2 * place(xh, f) + r, c, h, f, x))
        for f, xh, r, c, h, x in every(2, 4, 2, 2, 2, 4)
    ]


def final_moves(flip):
    moves = []
    for o, r, s, yh, x, xh in every(2, 2, 2, 2, 4, 4):
        c, low = divmod(place(xh, yh), 2)
        moves.append(
            (
                linear(4 * o + 2 * low + r, s ^ flip, c, yh, x),
                linear(4 * yh + xh, r, s, yh ^ o, x),
            )
        )
    return moves


def body(rollout_q, rollout_k, rollout_v, q_gain, k_gain, out_weight, cotangent, lengths, source):
    z, yl, c, yh, x = (lax.axis_index(name) for name in ALL)
    dp = (z * 2 + yl) * 2 + c
    shards = 32

    core = c.astype(jnp.int32)[None]
    w_chip = pair_of(core, out_weight, shift(out_weight, "c", 1))

    w_moved = lax.ppermute(w_chip, ALL, weight_moves())

    names = ("z", "yl", "c")
    to_right, to_left, scalars = edges(
        dp.astype(jnp.int32)[None], lengths, source, rollout_q, rollout_k, rollout_v, w_chip
    )
    left = lax.ppermute(to_right, names, [(i, i + 1) for i in range(shards - 1)])
    right = lax.ppermute(to_left, names, [(i, i - 1) for i in range(1, shards)])

    slots = [place((x + k) % 4, yh) for k in range(4)]
    mid = TOK // 2
    after, before = shift(cotangent, "x", -1), shift(cotangent, "x", 1)
    across = (shift(after[:mid], "x", -1), shift(before[mid:], "x", 1))
    cots = jnp.zeros((TOK, 2560), BF)
    for k, part in ((0, cotangent), (1, after), (3, before)):
        cots = lax.dynamic_update_slice(cots, part, (0, 640 * slots[k]))
    for row, part in zip((0, mid), across):
        cots = lax.dynamic_update_slice(cots, part, (row, 640 * slots[2]))

    qg = q_gain.reshape(1, HEAD)
    kg = k_gain.reshape(1, HEAD)
    packed, probs, att = forward(
        scalars, left, rollout_q, rollout_k, rollout_v, right, qg, kg
    )
    att_far = shift(att, "yh", 1)

    w_m = lax.all_gather(w_moved, "z", axis=0, tiled=True)
    w_o = shift(w_m, "c", 1)

    grad_scale = (TOK * shards) ** (-0.5)
    cots_send = lax.dynamic_slice_in_dim(cots, 1280 * (1 - c), 1280, 1)
    cots_keep = lax.dynamic_slice_in_dim(cots, 1280 * c, 1280, 1)

    def half(columns, rows):
        return (product(columns, rows, 0, 0) * grad_scale).astype(BF)

    both = jnp.concatenate([att, att_far], axis=1)
    got = shift(half(cots_send, both), "c", 1)
    keep = half(cots_keep, both)
    sums = (keep.astype(F32) + hold(got, w_m).astype(F32)).astype(BF)
    sums = jnp.concatenate([sums[:, :512], sums[:, 512:]], axis=0)
    summed = lax.psum_scatter(sums, "z", scatter_dimension=0, tiled=True)

    same = yh == c
    part_m = product(cots, w_m, 1, 0).astype(BF)
    part_o = product(cots, w_o, 1, 0).astype(BF)
    got_yh = shift(jnp.where(same, part_o, part_m), "yh", 1)
    att_m = jnp.where(same, att, att_far)
    att_o = jnp.where(same, att_far, att)

    def layer(k):
        rows_m = lax.dynamic_slice_in_dim(w_m, 640 * slots[k], 640, 0)
        rows_o = lax.dynamic_slice_in_dim(w_o, 640 * slots[k], 640, 0)
        return product(att_m, rows_m, 1, 1) + product(att_o, rows_o, 1, 1)

    opposite = layer(2).astype(BF)
    up = shift(opposite[:mid], "x", 1).astype(F32)
    down = shift(opposite[mid:], "x", -1).astype(F32)
    up = (layer(1) + jnp.pad(up, ((0, mid), (0, 0)))).astype(BF)
    down = (layer(3) + jnp.pad(down, ((mid, 0), (0, 0)))).astype(BF)
    last = down
    got = [shift(up, "x", 1).astype(F32), shift(down, "x", -1).astype(F32)]
    layer_out = (layer(0) + got[0] + got[1]).astype(BF)

    ready = halves_of(yl.astype(jnp.int32)[None], summed, last)
    query_grad, key_grad, value_grad = backward(
        same.astype(jnp.int32)[None], part_m, part_o, got_yh, packed, probs, qg, kg
    )
    landed = [lax.ppermute(ready[flip], ALL, final_moves(flip)) for flip in (0, 1)]
    weight_grad = landed[0].astype(F32) + landed[1].astype(F32)
    return layer_out, query_grad, key_grad, value_grad, weight_grad


def solution(mesh):
    grid = Mesh(mesh.devices.reshape(SIZES), ALL)
    dp, tensor = ("z", "yl", "c"), ("yh", "x")
    two = P(dp, tensor)
    return jax.shard_map(
        body,
        mesh=grid,
        in_specs=(two, two, two, P(), P(), two, two, P(), P()),
        out_specs=(two,) * 5,
        check_vma=False,
    )
```

```python
import functools
import itertools
import math

import jax
import jax.numpy as jnp
from jax import lax
from jax.experimental import pallas as pl
from jax.experimental.pallas import tpu as pltpu
from jax.sharding import Mesh, PartitionSpec as P

EPS = 1e-06
BF = jnp.bfloat16
F32 = jnp.float32
ALL = ("z", "yl", "c", "yh", "x")
SIZES = (8, 2, 2, 2, 4)
TOK = 672
EDGE = 208
ROWS = 1064
BLK = 112
WIN = 384
NBLK = TOK // BLK
SEQS = 6
HEAD = 128
HEADS = 4
SCALE = 1.0 / math.sqrt(HEAD)
VMEM = 56 * 1024 * 1024


def params():
    return pltpu.CompilerParams(vmem_limit_bytes=VMEM)


def cost(flops, nbytes):
    return pl.CostEstimate(flops=int(flops), bytes_accessed=int(nbytes), transcendentals=0)


def window(i):
    return max(0, BLK * (i + 1) - WIN)


def dot(a, b, ca, cb):
    return lax.dot_general(a, b, (((ca,), (cb,)), ((), ())), preferred_element_type=F32)


def edge_kernel(place, lengths, source, q, k, v, after, to_right, to_left, sc, wide):
    me = place[0]
    first = SEQS * me
    count = lengths.shape[0]

    def held(i):
        j = jnp.clip(i, 0, count - 1)
        return jnp.where((i == j) & (source[j] == me), lengths[j], 0)

    before = held(first - 1)
    total = before
    for t in range(SEQS + 1):
        total = total + held(first + t)
    lead = jnp.where(source[first] < me, lengths[first], 0)
    sc[0] = EDGE + before - lead
    sc[1] = EDGE + total
    begin = jnp.int32(0)
    for t in range(SEQS):
        sc[2 + t] = begin
        begin = begin + lengths[first + t]

    tail = jnp.clip(total - EDGE, 0, ROWS - EDGE)
    for t in range(6):
        ref, at = (q, t) if t < 4 else ((k, 0) if t == 4 else (v, 0))
        wide[t, :, :] = ref[:, HEAD * at : HEAD * (at + 1)].astype(F32)
        to_right[:, HEAD * t : HEAD * (t + 1)] = wide[t, pl.ds(tail, EDGE), :].astype(BF)
    to_left[:, 0:512] = q[0:EDGE, :]
    to_left[:, 512:640] = k[0:EDGE, :]
    to_left[:, 640:768] = v[0:EDGE, :]


def edges(place, lengths, source, q, k, v, after):
    vm = pl.BlockSpec(memory_space=pltpu.VMEM)
    sm = pl.BlockSpec(memory_space=pltpu.SMEM)
    out = jax.ShapeDtypeStruct((EDGE, 768), BF)
    return pl.pallas_call(
        edge_kernel,
        out_shape=(out, out, jax.ShapeDtypeStruct((2 + SEQS,), jnp.int32)),
        in_specs=[sm, sm, sm, vm, vm, vm, pl.BlockSpec(memory_space=pl.ANY)],
        out_specs=(vm, vm, sm),
        scratch_shapes=[pltpu.VMEM((6, ROWS, HEAD), F32)],
        compiler_params=params(),
        cost_estimate=cost(1, 1),
    )(place, lengths, source, q, k, v, after)


def fwd_kernel(sc, left, q, k, v, right, qg, kg, pk, p_out, o_out, com, qn, kn, p_buf, sems):
    parts = ((q, 0, 4), (k, 4, 1), (v, 5, 1))
    for ref, at, count in parts:
        for t in range(count):
            lanes = slice(HEAD * t, HEAD * (t + 1))
            com[at + t, EDGE : EDGE + ROWS, :] = ref[:, lanes].astype(F32)
    for t in range(6):
        lanes = slice(HEAD * t, HEAD * (t + 1))
        com[t, 0:EDGE, :] = left[:, lanes].astype(F32)
        com[t, pl.ds(sc[1], EDGE), :] = right[:, lanes].astype(F32)
    for i in range(NBLK):
        r = slice(BLK * i, BLK * (i + 1))
        xs = [com[t, pl.ds(sc[0] + BLK * i, BLK), :] for t in range(6)]
        for t in range(6):
            pk[r, HEAD * t : HEAD * (t + 1)] = xs[t].astype(BF)
        for h in range(HEADS + 1):
            e = xs[h]
            ms = jnp.mean(e * e, axis=-1, keepdims=True)
            gain = qg[...] if h < HEADS else kg[...]
            n = (e * lax.rsqrt(ms + EPS) * gain).astype(BF)
            if h < HEADS:
                qn[r, HEAD * h : HEAD * (h + 1)] = n
            else:
                kn[r, :] = n
    for i in range(NBLK):
        r = slice(BLK * i, BLK * (i + 1))
        w = slice(window(i), window(i) + WIN)
        kw = kn[w, :]
        vw = pk[w, 640:768]
        qs = jnp.concatenate([qn[r, HEAD * h : HEAD * (h + 1)] for h in range(HEADS)], axis=0)
        s = dot(qs, kw, 1, 1)
        row = lax.broadcasted_iota(jnp.int32, (BLK, WIN), 0) + BLK * i
        col = lax.broadcasted_iota(jnp.int32, (BLK, WIN), 1) + window(i)
        line = lax.broadcasted_iota(jnp.int32, (BLK, 1), 0) + BLK * i
        begin = jnp.zeros((BLK, 1), jnp.int32)
        for j in range(1, SEQS):
            begin = jnp.where(line >= sc[2 + j], sc[2 + j], begin)
        ok = (col <= row) & (col >= begin)
        pbs = []
        for h in range(HEADS):
            sh = jnp.where(ok, s[BLK * h : BLK * (h + 1), :] * SCALE, -1e30)
            e = jnp.exp(sh - jnp.max(sh, axis=-1, keepdims=True))
            pr = e * (1.0 / jnp.sum(e, axis=-1, keepdims=True))
            p_buf[i, BLK * h : BLK * (h + 1), :] = pr
            pbs.append(pr.astype(BF))
        pltpu.make_async_copy(p_buf.at[i], p_out.at[i], sems.at[i]).start()
        o = dot(jnp.concatenate(pbs, axis=0), vw, 1, 0).astype(BF)
        for h in range(HEADS):
            o_out[r, HEAD * h : HEAD * (h + 1)] = o[BLK * h : BLK * (h + 1), :]
    for i in range(NBLK):
        pltpu.make_async_copy(p_buf.at[i], p_out.at[i], sems.at[i]).wait()


def forward(sc, left, q, k, v, right, qg, kg):
    vm = pl.BlockSpec(memory_space=pltpu.VMEM)
    return pl.pallas_call(
        fwd_kernel,
        out_shape=(
            jax.ShapeDtypeStruct((TOK, 768), BF),
            jax.ShapeDtypeStruct((NBLK, HEADS * BLK, WIN), F32),
            jax.ShapeDtypeStruct((TOK, 512), BF),
        ),
        in_specs=[pl.BlockSpec(memory_space=pltpu.SMEM)] + [vm] * 7,
        out_specs=(vm, pl.BlockSpec(memory_space=pl.ANY), vm),
        scratch_shapes=[
            pltpu.VMEM((6, EDGE + ROWS + EDGE + 8, HEAD), F32),
            pltpu.VMEM((TOK, 512), BF),
            pltpu.VMEM((TOK, HEAD), BF),
            pltpu.VMEM((NBLK, HEADS * BLK, WIN), F32),
            pltpu.SemaphoreType.DMA((NBLK,)),
        ],
        compiler_params=params(),
        cost_estimate=cost(3e10, 9e6),
    )(sc, left, q, k, v, right, qg, kg)


def norm_back(x, gain, dy):
    r = lax.rsqrt(jnp.mean(x * x, axis=-1, keepdims=True) + EPS)
    xh = x * r
    gd = gain * dy
    return r * (gd - xh * jnp.mean(xh * gd, axis=-1, keepdims=True))


def bwd_kernel(
    sel, gm, go, got, pk, p_in, qg, kg, dq, dk, dv, qn, kn, do, dk_acc, dv_acc, p_buf, sems
):
    for i in range(NBLK):
        pltpu.make_async_copy(p_in.at[i], p_buf.at[i], sems.at[i]).start()
    first = sel[0] == 1
    for i in range(NBLK):
        r = slice(BLK * i, BLK * (i + 1))
        for h in range(HEADS + 1):
            c = slice(HEAD * h, HEAD * (h + 1))
            e = pk[r, c].astype(F32)
            ms = jnp.mean(e * e, axis=-1, keepdims=True)
            gain = qg[...] if h < HEADS else kg[...]
            n = (e * lax.rsqrt(ms + EPS) * gain).astype(BF)
            if h < HEADS:
                qn[r, c] = n
                own = jnp.where(first, gm[r, c].astype(F32), go[r, c].astype(F32))
                do[r, c] = (own + got[r, c].astype(F32)).astype(BF)
            else:
                kn[r, :] = n
    dk_acc[...] = jnp.zeros_like(dk_acc)
    dv_acc[...] = jnp.zeros_like(dv_acc)
    for i in range(NBLK):
        r = slice(BLK * i, BLK * (i + 1))
        w = slice(window(i), window(i) + WIN)
        kw = kn[w, :]
        vw = pk[w, 640:768]
        qs = jnp.concatenate([qn[r, HEAD * h : HEAD * (h + 1)] for h in range(HEADS)], axis=0)
        ds_ = jnp.concatenate([do[r, HEAD * h : HEAD * (h + 1)] for h in range(HEADS)], axis=0)
        dp = dot(ds_, vw, 1, 1)
        pltpu.make_async_copy(p_in.at[i], p_buf.at[i], sems.at[i]).wait()
        dss, pbs = [], []
        for h in range(HEADS):
            rows = slice(BLK * h, BLK * (h + 1))
            pr = p_buf[i, rows, :]
            dph = dp[rows, :]
            delta = jnp.sum(pr * dph, axis=-1, keepdims=True)
            dss.append((pr * (dph - delta) * SCALE).astype(BF))
            pbs.append(pr.astype(BF))
        dsc = jnp.concatenate(dss, axis=0)
        pb = jnp.concatenate(pbs, axis=0)
        dv_acc[w, :] += dot(pb, ds_, 0, 0)
        dk_acc[w, :] += dot(dsc, qs, 0, 0)
        dqn = dot(dsc, kw, 1, 0)
        for h in range(HEADS):
            c = slice(HEAD * h, HEAD * (h + 1))
            x = pk[r, c].astype(F32)
            dq[r, c] = norm_back(x, qg[...], dqn[BLK * h : BLK * (h + 1), :]).astype(BF)
    for i in range(NBLK):
        r = slice(BLK * i, BLK * (i + 1))
        dk[r, :] = norm_back(pk[r, 512:640].astype(F32), kg[...], dk_acc[r, :]).astype(BF)
        dv[r, :] = dv_acc[r, :].astype(BF)


def backward(sel, gm, go, got, pk, p, qg, kg):
    vm = pl.BlockSpec(memory_space=pltpu.VMEM)
    return pl.pallas_call(
        bwd_kernel,
        out_shape=(
            jax.ShapeDtypeStruct((TOK, 512), BF),
            jax.ShapeDtypeStruct((TOK, HEAD), BF),
            jax.ShapeDtypeStruct((TOK, HEAD), BF),
        ),
        in_specs=[pl.BlockSpec(memory_space=pltpu.SMEM)]
        + [vm] * 4
        + [pl.BlockSpec(memory_space=pl.ANY), vm, vm],
        out_specs=(vm, vm, vm),
        scratch_shapes=[
            pltpu.VMEM((TOK, 512), BF),
            pltpu.VMEM((TOK, HEAD), BF),
            pltpu.VMEM((TOK, 512), BF),
            pltpu.VMEM((TOK, HEAD), F32),
            pltpu.VMEM((TOK, HEAD), F32),
            pltpu.VMEM((NBLK, HEADS * BLK, WIN), F32),
            pltpu.SemaphoreType.DMA((NBLK,)),
        ],
        compiler_params=params(),
        cost_estimate=cost(6e9, 9e6),
    )(sel, gm, go, got, pk, p, qg, kg)


def halves_kernel(swap, rows, after, out0, out1):
    low, high = rows[0:160, :], rows[160:320, :]
    first = swap[0] == 0
    out0[...] = jnp.where(first, low, high)
    out1[...] = jnp.where(first, high, low)


def halves_of(swap, rows, after):
    vm = pl.BlockSpec(memory_space=pltpu.VMEM)
    out = jax.ShapeDtypeStruct((160, 512), BF)
    return pl.pallas_call(
        halves_kernel,
        out_shape=(out, out),
        in_specs=[
            pl.BlockSpec(memory_space=pltpu.SMEM),
            vm,
            pl.BlockSpec(memory_space=pl.ANY),
        ],
        out_specs=(vm, vm),
        compiler_params=params(),
        cost_estimate=cost(160 * 512, 1e6),
    )(swap, rows, after)


def pair_kernel(swap, here, pair, out):
    first = swap[0] == 0
    out[0:160, :] = jnp.where(first, here[...], pair[...])
    out[160:320, :] = jnp.where(first, pair[...], here[...])


def pair_of(swap, here, pair):
    vm = pl.BlockSpec(memory_space=pltpu.VMEM)
    return pl.pallas_call(
        pair_kernel,
        out_shape=jax.ShapeDtypeStruct((320, 512), BF),
        in_specs=[pl.BlockSpec(memory_space=pltpu.SMEM), vm, vm],
        out_specs=vm,
        compiler_params=params(),
        cost_estimate=cost(1, 1),
    )(swap, here, pair)


def hold_kernel(*refs):
    pass


def hold(value, *after):
    return pl.pallas_call(
        hold_kernel,
        out_shape=jax.ShapeDtypeStruct(value.shape, value.dtype),
        in_specs=[pl.BlockSpec(memory_space=pl.ANY)] * (1 + len(after)),
        out_specs=pl.BlockSpec(memory_space=pl.ANY),
        input_output_aliases={0: 0},
        cost_estimate=cost(1, 1),
    )(value, *after)


def product(a, b, ca, cb):
    return lax.dot_general(a, b, (((ca,), (cb,)), ((), ())), preferred_element_type=F32)


def shift(value, axis, k):
    n = lax.axis_size(axis)
    return lax.ppermute(value, axis, [(i, (i + k) % n) for i in range(n)])


def linear(z, yl, c, yh, x):
    return (((z * 2 + yl) * 2 + c) * 2 + yh) * 4 + x


def every(*sizes):
    return list(itertools.product(*(range(n) for n in sizes)))


def place(xh, f):
    high = xh // 2
    return (2 * ((xh + high + f + 1) % 2)) + 1 - high


def weight_moves():
    return [
        (linear(4 * f + xh, r, c, h, x), linear(2 * place(xh, f) + r, c, h, f, x))
        for f, xh, r, c, h, x in every(2, 4, 2, 2, 2, 4)
    ]


def final_moves(flip):
    moves = []
    for o, r, s, yh, x, xh in every(2, 2, 2, 2, 4, 4):
        c, low = divmod(place(xh, yh), 2)
        moves.append(
            (
                linear(4 * o + 2 * low + r, s ^ flip, c, yh, x),
                linear(4 * yh + xh, r, s, yh ^ o, x),
            )
        )
    return moves


def body(rollout_q, rollout_k, rollout_v, q_gain, k_gain, out_weight, cotangent, lengths, source):
    z, yl, c, yh, x = (lax.axis_index(name) for name in ALL)
    dp = (z * 2 + yl) * 2 + c
    shards = 32

    core = c.astype(jnp.int32)[None]
    w_chip = pair_of(core, out_weight, shift(out_weight, "c", 1))

    w_moved = lax.ppermute(w_chip, ALL, weight_moves())

    names = ("z", "yl", "c")
    to_right, to_left, scalars = edges(
        dp.astype(jnp.int32)[None], lengths, source, rollout_q, rollout_k, rollout_v, w_chip
    )
    left = lax.ppermute(to_right, names, [(i, i + 1) for i in range(shards - 1)])
    right = lax.ppermute(to_left, names, [(i, i - 1) for i in range(1, shards)])

    slots = [place((x + k) % 4, yh) for k in range(4)]
    mid = TOK // 2
    after, before = shift(cotangent, "x", -1), shift(cotangent, "x", 1)
    across = (shift(after[:mid], "x", -1), shift(before[mid:], "x", 1))
    cots = jnp.zeros((TOK, 2560), BF)
    for k, part in ((0, cotangent), (1, after), (3, before)):
        cots = lax.dynamic_update_slice(cots, part, (0, 640 * slots[k]))
    for row, part in zip((0, mid), across):
        cots = lax.dynamic_update_slice(cots, part, (row, 640 * slots[2]))

    qg = q_gain.reshape(1, HEAD)
    kg = k_gain.reshape(1, HEAD)
    packed, probs, att = forward(
        scalars, left, rollout_q, rollout_k, rollout_v, right, qg, kg
    )
    att_far = shift(att, "yh", 1)

    w_m = lax.all_gather(w_moved, "z", axis=0, tiled=True)
    w_o = shift(w_m, "c", 1)

    grad_scale = (TOK * shards) ** (-0.5)
    cots_send = lax.dynamic_slice_in_dim(cots, 1280 * (1 - c), 1280, 1)
    cots_keep = lax.dynamic_slice_in_dim(cots, 1280 * c, 1280, 1)

    def half(columns, rows):
        return (product(columns, rows, 0, 0) * grad_scale).astype(BF)

    both = jnp.concatenate([att, att_far], axis=1)
    got = shift(half(cots_send, both), "c", 1)
    keep = half(cots_keep, both)
    sums = (keep.astype(F32) + hold(got, w_m).astype(F32)).astype(BF)
    sums = jnp.concatenate([sums[:, :512], sums[:, 512:]], axis=0)
    summed = lax.psum_scatter(sums, "z", scatter_dimension=0, tiled=True)

    same = yh == c
    part_m = product(cots, w_m, 1, 0).astype(BF)
    part_o = product(cots, w_o, 1, 0).astype(BF)
    got_yh = shift(jnp.where(same, part_o, part_m), "yh", 1)
    att_m = jnp.where(same, att, att_far)
    att_o = jnp.where(same, att_far, att)

    def layer(k):
        rows_m = lax.dynamic_slice_in_dim(w_m, 640 * slots[k], 640, 0)
        rows_o = lax.dynamic_slice_in_dim(w_o, 640 * slots[k], 640, 0)
        return product(att_m, rows_m, 1, 1) + product(att_o, rows_o, 1, 1)

    opposite = layer(2).astype(BF)
    own = layer(0)
    up = hold(shift(opposite[:mid], "x", 1), own).astype(F32)
    down = shift(opposite[mid:], "x", -1).astype(F32)
    up = (layer(1) + jnp.pad(up, ((0, mid), (0, 0)))).astype(BF)
    down = (layer(3) + jnp.pad(down, ((mid, 0), (0, 0)))).astype(BF)
    last = down
    got = [shift(up, "x", 1).astype(F32), shift(down, "x", -1).astype(F32)]
    layer_out = (own + got[0] + got[1]).astype(BF)

    ready = halves_of(yl.astype(jnp.int32)[None], summed, last)
    query_grad, key_grad, value_grad = backward(
        same.astype(jnp.int32)[None], part_m, part_o, got_yh, packed, probs, qg, kg
    )
    landed = [lax.ppermute(ready[flip], ALL, final_moves(flip)) for flip in (0, 1)]
    weight_grad = landed[0].astype(F32) + landed[1].astype(F32)
    return layer_out, query_grad, key_grad, value_grad, weight_grad


def solution(mesh):
    grid = Mesh(mesh.devices.reshape(SIZES), ALL)
    dp, tensor = ("z", "yl", "c"), ("yh", "x")
    two = P(dp, tensor)
    return jax.shard_map(
        body,
        mesh=grid,
        in_specs=(two, two, two, P(), P(), two, two, P(), P()),
        out_specs=(two,) * 5,
        check_vma=False,
    )
```

```python
import functools
import itertools
import math

import jax
import jax.numpy as jnp
from jax import lax
from jax.experimental import pallas as pl
from jax.experimental.pallas import tpu as pltpu
from jax.sharding import Mesh, PartitionSpec as P

EPS = 1e-06
BF = jnp.bfloat16
F32 = jnp.float32
ALL = ("z", "yl", "c", "yh", "x")
SIZES = (8, 2, 2, 2, 4)
TOK = 672
EDGE = 208
ROWS = 1064
BLK = 112
WIN = 384
NBLK = TOK // BLK
SEQS = 6
HEAD = 128
HEADS = 4
SCALE = 1.0 / math.sqrt(HEAD)
VMEM = 56 * 1024 * 1024


def params():
    return pltpu.CompilerParams(vmem_limit_bytes=VMEM)


def cost(flops, nbytes):
    return pl.CostEstimate(flops=int(flops), bytes_accessed=int(nbytes), transcendentals=0)


def window(i):
    return max(0, BLK * (i + 1) - WIN)


def dot(a, b, ca, cb):
    return lax.dot_general(a, b, (((ca,), (cb,)), ((), ())), preferred_element_type=F32)


def edge_kernel(place, lengths, source, q, k, v, after, to_right, to_left, sc, wide):
    me = place[0]
    first = SEQS * me
    count = lengths.shape[0]

    def held(i):
        j = jnp.clip(i, 0, count - 1)
        return jnp.where((i == j) & (source[j] == me), lengths[j], 0)

    before = held(first - 1)
    total = before
    for t in range(SEQS + 1):
        total = total + held(first + t)
    lead = jnp.where(source[first] < me, lengths[first], 0)
    sc[0] = EDGE + before - lead
    sc[1] = EDGE + total
    begin = jnp.int32(0)
    for t in range(SEQS):
        sc[2 + t] = begin
        begin = begin + lengths[first + t]

    tail = jnp.clip(total - EDGE, 0, ROWS - EDGE)
    for t in range(6):
        ref, at = (q, t) if t < 4 else ((k, 0) if t == 4 else (v, 0))
        wide[t, :, :] = ref[:, HEAD * at : HEAD * (at + 1)].astype(F32)
        to_right[:, HEAD * t : HEAD * (t + 1)] = wide[t, pl.ds(tail, EDGE), :].astype(BF)
    to_left[:, 0:512] = q[0:EDGE, :]
    to_left[:, 512:640] = k[0:EDGE, :]
    to_left[:, 640:768] = v[0:EDGE, :]


def edges(place, lengths, source, q, k, v, after):
    vm = pl.BlockSpec(memory_space=pltpu.VMEM)
    sm = pl.BlockSpec(memory_space=pltpu.SMEM)
    out = jax.ShapeDtypeStruct((EDGE, 768), BF)
    return pl.pallas_call(
        edge_kernel,
        out_shape=(out, out, jax.ShapeDtypeStruct((2 + SEQS,), jnp.int32)),
        in_specs=[sm, sm, sm, vm, vm, vm, pl.BlockSpec(memory_space=pl.ANY)],
        out_specs=(vm, vm, sm),
        scratch_shapes=[pltpu.VMEM((6, ROWS, HEAD), F32)],
        compiler_params=params(),
        cost_estimate=cost(1, 1),
    )(place, lengths, source, q, k, v, after)


def fwd_kernel(sc, left, q, k, v, right, qg, kg, pk, p_out, o_out, com, qn, kn, p_buf, sems):
    parts = ((q, 0, 4), (k, 4, 1), (v, 5, 1))
    for ref, at, count in parts:
        for t in range(count):
            lanes = slice(HEAD * t, HEAD * (t + 1))
            com[at + t, EDGE : EDGE + ROWS, :] = ref[:, lanes].astype(F32)
    for t in range(6):
        lanes = slice(HEAD * t, HEAD * (t + 1))
        com[t, 0:EDGE, :] = left[:, lanes].astype(F32)
        com[t, pl.ds(sc[1], EDGE), :] = right[:, lanes].astype(F32)
    for i in range(NBLK):
        r = slice(BLK * i, BLK * (i + 1))
        xs = [com[t, pl.ds(sc[0] + BLK * i, BLK), :] for t in range(6)]
        for t in range(6):
            pk[r, HEAD * t : HEAD * (t + 1)] = xs[t].astype(BF)
        for h in range(HEADS + 1):
            e = xs[h]
            ms = jnp.mean(e * e, axis=-1, keepdims=True)
            gain = qg[...] if h < HEADS else kg[...]
            n = (e * lax.rsqrt(ms + EPS) * gain).astype(BF)
            if h < HEADS:
                qn[r, HEAD * h : HEAD * (h + 1)] = n
            else:
                kn[r, :] = n
    for i in range(NBLK):
        r = slice(BLK * i, BLK * (i + 1))
        w = slice(window(i), window(i) + WIN)
        kw = kn[w, :]
        vw = pk[w, 640:768]
        qs = jnp.concatenate([qn[r, HEAD * h : HEAD * (h + 1)] for h in range(HEADS)], axis=0)
        s = dot(qs, kw, 1, 1)
        row = lax.broadcasted_iota(jnp.int32, (BLK, WIN), 0) + BLK * i
        col = lax.broadcasted_iota(jnp.int32, (BLK, WIN), 1) + window(i)
        line = lax.broadcasted_iota(jnp.int32, (BLK, 1), 0) + BLK * i
        begin = jnp.zeros((BLK, 1), jnp.int32)
        for j in range(1, SEQS):
            begin = jnp.where(line >= sc[2 + j], sc[2 + j], begin)
        ok = (col <= row) & (col >= begin)
        pbs = []
        for h in range(HEADS):
            sh = jnp.where(ok, s[BLK * h : BLK * (h + 1), :] * SCALE, -1e30)
            e = jnp.exp(sh - jnp.max(sh, axis=-1, keepdims=True))
            pr = e * (1.0 / jnp.sum(e, axis=-1, keepdims=True))
            p_buf[i, BLK * h : BLK * (h + 1), :] = pr
            pbs.append(pr.astype(BF))
        pltpu.make_async_copy(p_buf.at[i], p_out.at[i], sems.at[i]).start()
        o = dot(jnp.concatenate(pbs, axis=0), vw, 1, 0).astype(BF)
        for h in range(HEADS):
            o_out[r, HEAD * h : HEAD * (h + 1)] = o[BLK * h : BLK * (h + 1), :]
    for i in range(NBLK):
        pltpu.make_async_copy(p_buf.at[i], p_out.at[i], sems.at[i]).wait()


def forward(sc, left, q, k, v, right, qg, kg):
    vm = pl.BlockSpec(memory_space=pltpu.VMEM)
    return pl.pallas_call(
        fwd_kernel,
        out_shape=(
            jax.ShapeDtypeStruct((TOK, 768), BF),
            jax.ShapeDtypeStruct((NBLK, HEADS * BLK, WIN), F32),
            jax.ShapeDtypeStruct((TOK, 512), BF),
        ),
        in_specs=[pl.BlockSpec(memory_space=pltpu.SMEM)] + [vm] * 7,
        out_specs=(vm, pl.BlockSpec(memory_space=pl.ANY), vm),
        scratch_shapes=[
            pltpu.VMEM((6, EDGE + ROWS + EDGE + 8, HEAD), F32),
            pltpu.VMEM((TOK, 512), BF),
            pltpu.VMEM((TOK, HEAD), BF),
            pltpu.VMEM((NBLK, HEADS * BLK, WIN), F32),
            pltpu.SemaphoreType.DMA((NBLK,)),
        ],
        compiler_params=params(),
        cost_estimate=cost(3e10, 9e6),
    )(sc, left, q, k, v, right, qg, kg)


def norm_back(x, gain, dy):
    r = lax.rsqrt(jnp.mean(x * x, axis=-1, keepdims=True) + EPS)
    xh = x * r
    gd = gain * dy
    return r * (gd - xh * jnp.mean(xh * gd, axis=-1, keepdims=True))


def bwd_kernel(
    mine, got, pk, p_in, qg, kg, dq, dk, dv, qn, kn, do, dk_acc, dv_acc, p_buf, sems
):
    for i in range(NBLK):
        pltpu.make_async_copy(p_in.at[i], p_buf.at[i], sems.at[i]).start()
    for i in range(NBLK):
        r = slice(BLK * i, BLK * (i + 1))
        for h in range(HEADS + 1):
            c = slice(HEAD * h, HEAD * (h + 1))
            e = pk[r, c].astype(F32)
            ms = jnp.mean(e * e, axis=-1, keepdims=True)
            gain = qg[...] if h < HEADS else kg[...]
            n = (e * lax.rsqrt(ms + EPS) * gain).astype(BF)
            if h < HEADS:
                qn[r, c] = n
                do[r, c] = (mine[r, c].astype(F32) + got[r, c].astype(F32)).astype(BF)
            else:
                kn[r, :] = n
    dk_acc[...] = jnp.zeros_like(dk_acc)
    dv_acc[...] = jnp.zeros_like(dv_acc)
    for i in range(NBLK):
        r = slice(BLK * i, BLK * (i + 1))
        w = slice(window(i), window(i) + WIN)
        kw = kn[w, :]
        vw = pk[w, 640:768]
        qs = jnp.concatenate([qn[r, HEAD * h : HEAD * (h + 1)] for h in range(HEADS)], axis=0)
        ds_ = jnp.concatenate([do[r, HEAD * h : HEAD * (h + 1)] for h in range(HEADS)], axis=0)
        dp = dot(ds_, vw, 1, 1)
        pltpu.make_async_copy(p_in.at[i], p_buf.at[i], sems.at[i]).wait()
        dss, pbs = [], []
        for h in range(HEADS):
            rows = slice(BLK * h, BLK * (h + 1))
            pr = p_buf[i, rows, :]
            dph = dp[rows, :]
            delta = jnp.sum(pr * dph, axis=-1, keepdims=True)
            dss.append((pr * (dph - delta) * SCALE).astype(BF))
            pbs.append(pr.astype(BF))
        dsc = jnp.concatenate(dss, axis=0)
        pb = jnp.concatenate(pbs, axis=0)
        dv_acc[w, :] += dot(pb, ds_, 0, 0)
        dk_acc[w, :] += dot(dsc, qs, 0, 0)
        dqn = dot(dsc, kw, 1, 0)
        for h in range(HEADS):
            c = slice(HEAD * h, HEAD * (h + 1))
            x = pk[r, c].astype(F32)
            dq[r, c] = norm_back(x, qg[...], dqn[BLK * h : BLK * (h + 1), :]).astype(BF)
    for i in range(NBLK):
        r = slice(BLK * i, BLK * (i + 1))
        dk[r, :] = norm_back(pk[r, 512:640].astype(F32), kg[...], dk_acc[r, :]).astype(BF)
        dv[r, :] = dv_acc[r, :].astype(BF)


def backward(mine, got, pk, p, qg, kg):
    vm = pl.BlockSpec(memory_space=pltpu.VMEM)
    return pl.pallas_call(
        bwd_kernel,
        out_shape=(
            jax.ShapeDtypeStruct((TOK, 512), BF),
            jax.ShapeDtypeStruct((TOK, HEAD), BF),
            jax.ShapeDtypeStruct((TOK, HEAD), BF),
        ),
        in_specs=[vm] * 3 + [pl.BlockSpec(memory_space=pl.ANY), vm, vm],
        out_specs=(vm, vm, vm),
        scratch_shapes=[
            pltpu.VMEM((TOK, 512), BF),
            pltpu.VMEM((TOK, HEAD), BF),
            pltpu.VMEM((TOK, 512), BF),
            pltpu.VMEM((TOK, HEAD), F32),
            pltpu.VMEM((TOK, HEAD), F32),
            pltpu.VMEM((NBLK, HEADS * BLK, WIN), F32),
            pltpu.SemaphoreType.DMA((NBLK,)),
        ],
        compiler_params=params(),
        cost_estimate=cost(6e9, 9e6),
    )(mine, got, pk, p, qg, kg)


def halves_kernel(swap, rows, after, out0, out1):
    low, high = rows[0:160, :], rows[160:320, :]
    first = swap[0] == 0
    out0[...] = jnp.where(first, low, high)
    out1[...] = jnp.where(first, high, low)


def halves_of(swap, rows, after):
    vm = pl.BlockSpec(memory_space=pltpu.VMEM)
    out = jax.ShapeDtypeStruct((160, 512), BF)
    return pl.pallas_call(
        halves_kernel,
        out_shape=(out, out),
        in_specs=[
            pl.BlockSpec(memory_space=pltpu.SMEM),
            vm,
            pl.BlockSpec(memory_space=pl.ANY),
        ],
        out_specs=(vm, vm),
        compiler_params=params(),
        cost_estimate=cost(160 * 512, 1e6),
    )(swap, rows, after)


def hold_kernel(*refs):
    pass


def hold(value, *after):
    return pl.pallas_call(
        hold_kernel,
        out_shape=jax.ShapeDtypeStruct(value.shape, value.dtype),
        in_specs=[pl.BlockSpec(memory_space=pl.ANY)] * (1 + len(after)),
        out_specs=pl.BlockSpec(memory_space=pl.ANY),
        input_output_aliases={0: 0},
        cost_estimate=cost(1, 1),
    )(value, *after)


def product(a, b, ca, cb):
    return lax.dot_general(a, b, (((ca,), (cb,)), ((), ())), preferred_element_type=F32)


def shift(value, axis, k):
    n = lax.axis_size(axis)
    return lax.ppermute(value, axis, [(i, (i + k) % n) for i in range(n)])


def linear(z, yl, c, yh, x):
    return (((z * 2 + yl) * 2 + c) * 2 + yh) * 4 + x


def every(*sizes):
    return list(itertools.product(*(range(n) for n in sizes)))


def place(xh, f):
    high = xh // 2
    return (2 * ((xh + high + f + 1) % 2)) + 1 - high


def weight_moves():
    return [
        (linear(4 * f + xh, r, c, h, x), linear(2 * place(xh, f) + r, c, h, f, x))
        for f, xh, r, c, h, x in every(2, 4, 2, 2, 2, 4)
    ]


def final_moves(flip):
    moves = []
    for o, r, s, yh, x, xh in every(2, 2, 2, 2, 4, 4):
        c, low = divmod(place(xh, yh), 2)
        moves.append(
            (
                linear(4 * o + 2 * low + r, s ^ flip, c, yh, x),
                linear(4 * yh + xh, r, s, yh ^ o, x),
            )
        )
    return moves


def body(rollout_q, rollout_k, rollout_v, q_gain, k_gain, out_weight, cotangent, lengths, source):
    z, yl, c, yh, x = (lax.axis_index(name) for name in ALL)
    dp = (z * 2 + yl) * 2 + c
    shards = 32

    w_pair = shift(out_weight, "c", 1)
    w_chip = jnp.where(
        c == 0,
        jnp.concatenate([out_weight, w_pair], axis=0),
        jnp.concatenate([w_pair, out_weight], axis=0),
    )

    w_moved = lax.ppermute(w_chip, ALL, weight_moves())

    names = ("z", "yl", "c")
    to_right, to_left, scalars = edges(
        dp.astype(jnp.int32)[None], lengths, source, rollout_q, rollout_k, rollout_v, w_chip
    )
    left = lax.ppermute(to_right, names, [(i, i + 1) for i in range(shards - 1)])
    right = lax.ppermute(to_left, names, [(i, i - 1) for i in range(1, shards)])

    slots = [place((x + k) % 4, yh) for k in range(4)]
    mid = TOK // 2
    after, before = shift(cotangent, "x", -1), shift(cotangent, "x", 1)
    across = (shift(after[:mid], "x", -1), shift(before[mid:], "x", 1))
    cots = jnp.zeros((TOK, 2560), BF)
    for k, part in ((0, cotangent), (1, after), (3, before)):
        cots = lax.dynamic_update_slice(cots, part, (0, 640 * slots[k]))
    for row, part in zip((0, mid), across):
        cots = lax.dynamic_update_slice(cots, part, (row, 640 * slots[2]))

    qg = q_gain.reshape(1, HEAD)
    kg = k_gain.reshape(1, HEAD)
    packed, probs, att = forward(
        scalars, left, rollout_q, rollout_k, rollout_v, right, qg, kg
    )
    att_far = shift(att, "yh", 1)

    w_m = lax.all_gather(w_moved, "z", axis=0, tiled=True)
    w_o = shift(w_m, "c", 1)

    grad_scale = (TOK * shards) ** (-0.5)
    cots_send = lax.dynamic_slice_in_dim(cots, 1280 * (1 - c), 1280, 1)
    cots_keep = lax.dynamic_slice_in_dim(cots, 1280 * c, 1280, 1)

    def half(columns, rows):
        return (product(columns, rows, 0, 0) * grad_scale).astype(BF)

    both = jnp.concatenate([att, att_far], axis=1)
    got = shift(half(cots_send, both), "c", 1)
    keep = half(cots_keep, both)
    sums = (keep.astype(F32) + hold(got, w_m).astype(F32)).astype(BF)
    sums = jnp.concatenate([sums[:, :512], sums[:, 512:]], axis=0)
    summed = lax.psum_scatter(sums, "z", scatter_dimension=0, tiled=True)

    same = yh == c
    part_m = product(cots, w_m, 1, 0).astype(BF)
    part_o = product(cots, w_o, 1, 0).astype(BF)
    got_yh = shift(jnp.where(same, part_o, part_m), "yh", 1)
    att_m = jnp.where(same, att, att_far)
    att_o = jnp.where(same, att_far, att)

    def layer(k):
        rows_m = lax.dynamic_slice_in_dim(w_m, 640 * slots[k], 640, 0)
        rows_o = lax.dynamic_slice_in_dim(w_o, 640 * slots[k], 640, 0)
        return product(att_m, rows_m, 1, 1) + product(att_o, rows_o, 1, 1)

    opposite = layer(2).astype(BF)
    own = layer(0)
    up = hold(shift(opposite[:mid], "x", 1), own).astype(F32)
    down = shift(opposite[mid:], "x", -1).astype(F32)
    up = (layer(1) + jnp.pad(up, ((0, mid), (0, 0)))).astype(BF)
    down = (layer(3) + jnp.pad(down, ((mid, 0), (0, 0)))).astype(BF)
    last = down
    got = [shift(up, "x", 1).astype(F32), shift(down, "x", -1).astype(F32)]
    layer_out = (own + got[0] + got[1]).astype(BF)

    ready = halves_of(yl.astype(jnp.int32)[None], summed, last)
    query_grad, key_grad, value_grad = backward(
        jnp.where(same, part_m, part_o), got_yh, packed, probs, qg, kg
    )
    landed = [lax.ppermute(ready[flip], ALL, final_moves(flip)) for flip in (0, 1)]
    weight_grad = landed[0].astype(F32) + landed[1].astype(F32)
    return layer_out, query_grad, key_grad, value_grad, weight_grad


def solution(mesh):
    grid = Mesh(mesh.devices.reshape(SIZES), ALL)
    dp, tensor = ("z", "yl", "c"), ("yh", "x")
    two = P(dp, tensor)
    return jax.shard_map(
        body,
        mesh=grid,
        in_specs=(two, two, two, P(), P(), two, two, P(), P()),
        out_specs=(two,) * 5,
        check_vma=False,
    )
```
